32 devices in a mesh: row: 8 (over y, x, core), col: 4 (over z).
Axes of the slice: x: 2, y: 2, z: 4, core: 2. Of those that a mesh axis runs over, the one named last changes fastest.
Arguments:
- integrals: bfloat16 [8192, 1024], P('row', 'col'), may hold values from -6 to 6
- amplitudes: bfloat16 [1024, 6144], P('row', 'col'), may hold values from -0.5 to 0.5
- screen: int32 [8, 48], P('row', 'col'), may hold values from 0 to 1, as said below
- next_owner: int32 [64], replicated, may hold values from 0 to 7, as said below
Outputs:
- regrouped: bfloat16 [8192, 6144], P('row', 'col')
The draws below stay inside these ranges and needn't reach their ends.
Inputs may be any that keep to these rules, and one draw needn't show every extreme that they name: In each aligned block of 1 x 12 tiles of screen (one device's block), between 1 and 2 entries are 1; some block holds exactly 2. next_owner[p * 8 + s] equals p XOR m_s, where m_s (0 to 7) depends only on s.
All inputs are finite; a program needn't handle non-finite values.
Results may differ from the reference program's by a relative error of at most 0.001.
Values may be sent and summed in bfloat16 or wider, within the bound.
A program may use at most 128 MiB of HBM per device.

```python
import jax
import jax.numpy as jnp
from jax import lax

TILE = 128
ROW_TILES = 8
COL_TILES = 12
K_TILES = 1
CAP = 2
ROWS_ALL = 8192
DEPTH = 1024
WIDTH = 6144
N_ROW = 8
N_COL = 4


def draw_screen(key, part):
    key = jax.random.fold_in(key, 7)
    block_count = N_ROW * N_COL
    cell_count = K_TILES * COL_TILES
    key_counts, key_full, key_order = jax.random.split(key, 3)
    counts = jax.random.randint(key_counts, (block_count,), 1, CAP + 1)
    fullest = jax.random.randint(key_full, (), 0, block_count)
    counts = jnp.where(jnp.arange(block_count) == fullest, CAP, counts)
    block_keys = jax.random.split(key_order, block_count)
    orders = jax.vmap(lambda single: jax.random.permutation(single, cell_count))(block_keys)
    flags = (orders < counts[:, None]).astype(jnp.int32)
    flags = flags.reshape(N_ROW, N_COL, K_TILES, COL_TILES).transpose(0, 2, 1, 3)
    return flags.reshape(N_ROW * K_TILES, N_COL * COL_TILES)


def draw_next_owner(key, part):
    key = jax.random.fold_in(key, 11)
    moves = jax.random.randint(key, (ROW_TILES,), 0, N_ROW)
    owners = jnp.bitwise_xor(jnp.arange(N_ROW, dtype=jnp.int32)[:, None], moves[None, :].astype(jnp.int32))
    return owners.reshape(N_ROW * ROW_TILES).astype(jnp.int32)


def shard_levels(stream_key, dims, cuts, smallest, high):
    level = 1.0
    for dim, blocks in cuts:
        steps = jax.random.uniform(jax.random.fold_in(jax.random.fold_in(stream_key, 6), dim), (blocks,), jnp.float32, smallest / len(cuts), high / len(cuts))
        level = level * jnp.repeat(jnp.exp(steps), dims[dim] // blocks).reshape((-1,) + (1,) * (len(dims) - 1 - dim))
    return level


def scatter_about(rng, dims, scale, bound, shards=(), held_as=jnp.bfloat16):
    drawn = jax.random.normal(rng, dims, jnp.float32) * scale
    if len(shards) > 0:
        drawn = shard_levels(rng, dims, shards, -0.22, 0.18) * drawn
    return jnp.clip(drawn, min=-bound, max=bound).astype(held_as)


def setup_inputs(seed: int = 0) -> dict:
    splits = jax.random.split(jax.random.key(seed), 5)
    return {
        "integrals": scatter_about(splits[0], (ROWS_ALL, DEPTH), 1.0, 6.0, ((0, 8), (1, 4))),
        "amplitudes": scatter_about(splits[1], (DEPTH, WIDTH), (max(TILE, TILE * N_ROW * (CAP + 1) // (2 * COL_TILES))) ** -0.5, 0.5, ((0, 8), (1, 4))),
        "screen": draw_screen(jax.random.fold_in(splits[4], 71), 0),
        "next_owner": draw_next_owner(jax.random.fold_in(splits[4], 71), 0),
    }


def reference(integrals, amplitudes, screen, next_owner):
    row_count = integrals.shape[0]
    col_width = amplitudes.shape[1]
    depth_tiles = screen.shape[0]
    width_tiles = screen.shape[1]
    order = jnp.arange(depth_tiles * width_tiles, dtype=jnp.int32)

    def step(total, position):
        depth_at = (position // width_tiles).astype(jnp.int32)
        width_at = (position % width_tiles).astype(jnp.int32)

        def add_tile(carried):
            left_block = lax.dynamic_slice_in_dim(integrals, depth_at * TILE, TILE, 1)
            right_block = lax.dynamic_slice(amplitudes, (depth_at * TILE, width_at * TILE), (TILE, TILE))
            before = lax.dynamic_slice_in_dim(carried, width_at * TILE, TILE, 1)
            after = before + jnp.dot(left_block, right_block, preferred_element_type=jnp.float32)
            return lax.dynamic_update_slice_in_dim(carried, after, width_at * TILE, 1)

        def keep_tile(carried):
            return carried

        return lax.cond(screen[depth_at, width_at] == 1, add_tile, keep_tile, total), None

    start_total = jnp.zeros((row_count, col_width), jnp.float32)
    product, unused = lax.scan(step, start_total, order)
    residual = product.astype(jnp.bfloat16)
    row_tiles_all = row_count // TILE
    tiled = residual.reshape(row_tiles_all, TILE, col_width)
    slot_index = jnp.arange(row_tiles_all, dtype=jnp.int32) % ROW_TILES
    new_place = (next_owner.astype(jnp.int32) * ROW_TILES + slot_index).astype(jnp.int32)
    moved = jnp.zeros_like(tiled).at[new_place].set(tiled)
    return moved.reshape(row_count, col_width)
```

```python
import functools

import jax
import jax.numpy as jnp
from jax import lax
from jax.experimental import pallas as pl
from jax.experimental.pallas import tpu as pltpu
from jax.sharding import PartitionSpec as P

TILE = 128
CAP = 2
PAIR = 2
MESH = pl.DeviceIdType.MESH


def kernel(
    n_row, n_col, n_raw,
    a_ref, amp_ref, scr_ref, own_ref, out_ref,
    G, X, F, RX, AG, W, O,
    zr_send, zr_recv, zl_send, zl_recv, p_send, p_recv, r_send, r_recv, a_send, a_recv, o_sem,
):
    p = lax.axis_index("row")
    c = lax.axis_index("col")
    bits = n_row.bit_length() - 1
    tiles = a_ref.shape[0] // TILE
    width_tiles = amp_ref.shape[1] // TILE

    def partner(b):
        mask = 2**b
        return p + mask - 2 * mask * ((p // mask) % 2)

    barrier = pltpu.get_barrier_semaphore()
    for b in range(bits):
        pl.semaphore_signal(barrier, inc=1, device_id={"row": partner(b)}, device_id_type=MESH)

    @pl.when(c > 0)
    def _():
        pl.semaphore_signal(barrier, inc=1, device_id={"col": c - 1}, device_id_type=MESH)

    @pl.when(c < n_col - 1)
    def _():
        pl.semaphore_signal(barrier, inc=1, device_id={"col": c + 1}, device_id_type=MESH)

    near = (c > 0).astype(jnp.int32) + (c < n_col - 1).astype(jnp.int32)
    pl.semaphore_wait(barrier, bits + near)

    def rows(s):
        return pl.ds(s * TILE, TILE)

    def z_copy(s, h, right, block):
        src = a_ref.at[rows(s)] if h == 0 and s < n_raw else G.at[block, rows(s)]
        send, recv = (zr_send, zr_recv) if right else (zl_send, zl_recv)
        return pltpu.make_async_remote_copy(
            src_ref=src,
            dst_ref=G.at[block, rows(s)],
            send_sem=send.at[s, h],
            recv_sem=recv.at[s, h],
            device_id={"col": c + 1 if right else c - 1},
            device_id_type=MESH,
        )

    def z_wait(s, h):
        @pl.when(c - 1 - h >= 0)
        def _():
            z_copy(s, h, True, c - 1 - h).wait_recv()

        @pl.when(c + 1 + h < n_col)
        def _():
            z_copy(s, h, False, c + 1 + h).wait_recv()

    def z_edges(s, h, act):
        @pl.when((c - h >= 0) & (c < n_col - 1))
        def _():
            act(z_copy(s, h, True, c - h))

        @pl.when((c + h < n_col) & (c > 0))
        def _():
            act(z_copy(s, h, False, c + h))

    def z_hop(s, h):
        if h > 0:
            z_wait(s, h - 1)
        z_edges(s, h, lambda copy: copy.start())

    def order(s):
        far = list(range(1, bits))
        turn = s % len(far)
        return far[turn:] + far[:turn] + [0]

    def flip(s, b):
        return (own_ref[s] // 2**b) % 2 == 1

    def p_copy(s, i):
        b = order(s)[i]
        src = a_ref.at[rows(s)] if i == 0 else G.at[c, rows(s)]
        return pltpu.make_async_remote_copy(
            src_ref=src,
            dst_ref=X.at[i, rows(s - n_raw)],
            send_sem=p_send.at[s - n_raw, i],
            recv_sem=p_recv.at[s - n_raw, i],
            device_id={"row": partner(b)},
            device_id_type=MESH,
        )

    def p_stage(s, i):
        if i > 0:
            copy = p_copy(s, i - 1)
            copy.wait_recv()
            copy.wait_send()
            mine = a_ref[rows(s)] if i == 1 else G[c, rows(s)]
            G[c, rows(s)] = jnp.where(flip(s, order(s)[i - 1]), X[i - 1, rows(s - n_raw)], mine)
        if i < bits:
            p_copy(s, i).start()

    def r_copy(s, i):
        b = order(s)[i]
        src = G.at[:, rows(s)] if i == 0 else F.at[:, rows(s)]
        return pltpu.make_async_remote_copy(
            src_ref=src,
            dst_ref=RX.at[i, :, rows(s)],
            send_sem=r_send.at[s, i],
            recv_sem=r_recv.at[s, i],
            device_id={"row": partner(b)},
            device_id_type=MESH,
        )

    def r_stage(s, i):
        if i == 0:
            G[c, rows(s)] = a_ref[rows(s)]
        if i > 0:
            copy = r_copy(s, i - 1)
            copy.wait_recv()
            copy.wait_send()
            flipped = flip(s, order(s)[i - 1])
            for k in range(n_col):
                mine = G[k, rows(s)] if i == 1 else F[k, rows(s)]
                F[k, rows(s)] = jnp.where(flipped, RX[i - 1, k, rows(s)], mine)
        if i < bits:
            r_copy(s, i).start()

    def pack():
        count = jnp.int32(0)
        place = [jnp.int32(0)] * CAP
        for j in range(width_tiles):
            flag = scr_ref[0, j]
            for i in range(CAP):
                here = flag * (count == i).astype(jnp.int32)
                place[i] = place[i] + here * (j + 1)
            count = count + flag
        at = lax.broadcasted_iota(jnp.int32, (16, TILE), 0) + 1
        for i in range(CAP):
            total = jnp.zeros((TILE, TILE), jnp.float32)
            for j in range(width_tiles):
                block = amp_ref[:, j * TILE:(j + 1) * TILE].astype(jnp.float32)
                total = jnp.where(place[i] == j + 1, block, total)
            AG[p, i * TILE:(i + 1) * TILE] = total.astype(jnp.bfloat16)
            mark = jnp.where(at == place[i], 1.0, 0.0)
            AG[p, CAP * TILE + i * 16:CAP * TILE + (i + 1) * 16] = mark.astype(jnp.bfloat16)

    def a_copy(b):
        size = 2**b
        block = pl.ds((p // size) * size, size)
        return pltpu.make_async_remote_copy(
            src_ref=AG.at[block],
            dst_ref=AG.at[block],
            send_sem=a_send.at[b],
            recv_sem=a_recv.at[b],
            device_id={"row": partner(b)},
            device_id_type=MESH,
        )

    def a_wait(b):
        size = 2**b
        other = pl.ds((partner(b) // size) * size, size)
        pltpu.make_async_remote_copy(
            src_ref=AG.at[other],
            dst_ref=AG.at[other],
            send_sem=a_send.at[b],
            recv_sem=a_recv.at[b],
            device_id={"row": partner(b)},
            device_id_type=MESH,
        ).wait_recv()

    def expand():
        def step(k, carry):
            first = AG[k, 0:TILE].astype(jnp.float32)
            second = AG[k, TILE:2 * TILE].astype(jnp.float32)
            marks = AG[k, 2 * TILE:2 * TILE + 32].astype(jnp.float32)
            at = pl.ds(pl.multiple_of(k * TILE, TILE), TILE)
            for j in range(width_tiles):
                value = first * marks[j:j + 1] + second * marks[16 + j:17 + j]
                W[at, j * TILE:(j + 1) * TILE] = value.astype(jnp.bfloat16)
            return carry

        lax.fori_loop(0, n_row, step, 0)

    depth = a_ref.shape[1]
    wide = 2 * TILE

    def o_copy(q):
        at = pl.ds(q * PAIR * TILE, PAIR * TILE)
        return pltpu.make_async_copy(O.at[at], out_ref.at[at], o_sem.at[q])

    def compute(q):
        at = pl.ds(q * PAIR * TILE, PAIR * TILE)
        held = F if q * PAIR < n_raw else G

        def step(n, carry):
            cols = pl.ds(pl.multiple_of(n * wide, wide), wide)
            total = jnp.zeros((PAIR * TILE, wide), jnp.float32)
            for k in range(n_col):
                total += jnp.dot(
                    held[k, at], W[k * depth:(k + 1) * depth, cols], preferred_element_type=jnp.float32
                )
            O[at, cols] = total.astype(jnp.bfloat16)
            return carry

        lax.fori_loop(0, amp_ref.shape[1] // wide, step, 0)
        o_copy(q).start()

    pairs = tiles // PAIR
    raw_pairs = n_raw // PAIR

    def pair(q):
        return range(q * PAIR, (q + 1) * PAIR)

    last = n_col - 1
    slots = pairs + bits + n_col + bits + 4
    a_next = 0
    for slot in range(slots):
        for q in range(pairs):
            enter = q if q < raw_pairs else q - raw_pairs + bits
            if q >= raw_pairs:
                i = slot - (q - raw_pairs)
                if 0 <= i <= bits:
                    for s in pair(q):
                        p_stage(s, i)
            h = slot - enter
            if 0 <= h < last:
                for s in pair(q):
                    z_hop(s, h)
            if h == last:
                for s in pair(q):
                    z_wait(s, last - 1)
            if q < raw_pairs:
                i = slot - (enter + last + 1)
                if 0 <= i <= bits:
                    for s in pair(q):
                        r_stage(s, i)
        if slot == 0:
            pack()
            a_copy(0).start()
        elif slot <= bits:
            a_wait(slot - 1)
            if slot < bits:
                a_copy(slot).start()
            else:
                expand()
        for q in range(pairs):
            ready = q + last + 1 + bits if q < raw_pairs else q - raw_pairs + bits + last
            if slot == max(ready, bits):
                compute(q)

    for s in range(tiles):
        for h in range(last):
            z_edges(s, h, lambda copy: copy.wait_send())
    for b in range(bits):
        a_copy(b).wait_send()
    for q in range(pairs):
        o_copy(q).wait()


def body(integrals, amplitudes, screen, next_owner):
    n_row, n_col = lax.axis_size("row"), lax.axis_size("col")
    bits = n_row.bit_length() - 1
    row_count, depth = integrals.shape
    width = amplitudes.shape[1]
    tiles = row_count // TILE
    n_raw = PAIR
    late = row_count - n_raw * TILE
    last = n_col - 1
    dma = pltpu.SemaphoreType.DMA
    vmem = pl.BlockSpec(memory_space=pltpu.VMEM)
    smem = pl.BlockSpec(memory_space=pltpu.SMEM)
    bf16 = jnp.bfloat16
    return pl.pallas_call(
        functools.partial(kernel, n_row, n_col, n_raw),
        out_shape=jax.ShapeDtypeStruct((row_count, width), bf16),
        in_specs=[vmem, vmem, smem, smem],
        out_specs=pl.BlockSpec(memory_space=pl.ANY),
        scratch_shapes=[
            pltpu.VMEM((n_col, row_count, depth), bf16),
            pltpu.VMEM((bits, late, depth), bf16),
            pltpu.VMEM((n_col, n_raw * TILE, depth), bf16),
            pltpu.VMEM((bits, n_col, n_raw * TILE, depth), bf16),
            pltpu.VMEM((n_row, CAP * TILE + 32, TILE), bf16),
            pltpu.VMEM((n_row * TILE, width), bf16),
            pltpu.VMEM((row_count, width), bf16),
            dma((tiles, last)),
            dma((tiles, last)),
            dma((tiles, last)),
            dma((tiles, last)),
            dma((tiles - n_raw, bits)),
            dma((tiles - n_raw, bits)),
            dma((n_raw, bits)),
            dma((n_raw, bits)),
            dma((bits,)),
            dma((bits,)),
            dma((tiles // PAIR,)),
        ],
        compiler_params=pltpu.CompilerParams(
            collective_id=0, has_side_effects=True, vmem_limit_bytes=56 * 1024 * 1024
        ),
    )(integrals, amplitudes, screen, next_owner)


def solution(mesh):
    placed = (P("row", "col"), P("row", "col"), P("row", "col"), P())
    return jax.shard_map(
        body, mesh=mesh, in_specs=placed, out_specs=P("row", "col"), check_vma=False
    )
```

```python
import functools

import jax
import jax.numpy as jnp
from jax import lax
from jax.experimental import pallas as pl
from jax.experimental.pallas import tpu as pltpu
from jax.sharding import PartitionSpec as P

TILE = 128
CAP = 2
PAIR = 2
MESH = pl.DeviceIdType.MESH


def kernel(
    n_row, n_col, n_raw,
    a_ref, amp_ref, scr_ref, own_ref, out_ref,
    G, X, F, RX, AG, W, O,
    zr_send, zr_recv, zl_send, zl_recv, p_send, p_recv, r_send, r_recv, a_send, a_recv, o_sem,
):
    p = lax.axis_index("row")
    c = lax.axis_index("col")
    bits = n_row.bit_length() - 1
    tiles = a_ref.shape[0] // TILE
    width_tiles = amp_ref.shape[1] // TILE

    def partner(b):
        mask = 2**b
        return p + mask - 2 * mask * ((p // mask) % 2)

    barrier = pltpu.get_barrier_semaphore()
    for b in range(bits):
        pl.semaphore_signal(barrier, inc=1, device_id={"row": partner(b)}, device_id_type=MESH)

    @pl.when(c > 0)
    def _():
        pl.semaphore_signal(barrier, inc=1, device_id={"col": c - 1}, device_id_type=MESH)

    @pl.when(c < n_col - 1)
    def _():
        pl.semaphore_signal(barrier, inc=1, device_id={"col": c + 1}, device_id_type=MESH)

    near = (c > 0).astype(jnp.int32) + (c < n_col - 1).astype(jnp.int32)
    pl.semaphore_wait(barrier, bits + near)

    def rows(s):
        return pl.ds(s * TILE, TILE)

    def z_copy(s, h, right, block):
        src = a_ref.at[rows(s)] if h == 0 and s < n_raw else G.at[block, rows(s)]
        send, recv = (zr_send, zr_recv) if right else (zl_send, zl_recv)
        return pltpu.make_async_remote_copy(
            src_ref=src,
            dst_ref=G.at[block, rows(s)],
            send_sem=send.at[s, h],
            recv_sem=recv.at[s, h],
            device_id={"col": c + 1 if right else c - 1},
            device_id_type=MESH,
        )

    def z_wait(s, h):
        @pl.when(c - 1 - h >= 0)
        def _():
            z_copy(s, h, True, c - 1 - h).wait_recv()

        @pl.when(c + 1 + h < n_col)
        def _():
            z_copy(s, h, False, c + 1 + h).wait_recv()

    def z_edges(s, h, act):
        @pl.when((c - h >= 0) & (c < n_col - 1))
        def _():
            act(z_copy(s, h, True, c - h))

        @pl.when((c + h < n_col) & (c > 0))
        def _():
            act(z_copy(s, h, False, c + h))

    def z_hop(s, h):
        if h > 0:
            z_wait(s, h - 1)
        z_edges(s, h, lambda copy: copy.start())

    def order(s):
        far = list(range(1, bits))
        turn = s % len(far)
        return far[turn:] + far[:turn] + [0]

    def flip(s, b):
        return (own_ref[s] // 2**b) % 2 == 1

    def p_copy(s, i):
        b = order(s)[i]
        src = a_ref.at[rows(s)] if i == 0 else G.at[c, rows(s)]
        return pltpu.make_async_remote_copy(
            src_ref=src,
            dst_ref=X.at[i, rows(s - n_raw)],
            send_sem=p_send.at[s - n_raw, i],
            recv_sem=p_recv.at[s - n_raw, i],
            device_id={"row": partner(b)},
            device_id_type=MESH,
        )

    def p_stage(s, i):
        if i > 0:
            copy = p_copy(s, i - 1)
            copy.wait_recv()
            copy.wait_send()
            mine = a_ref[rows(s)] if i == 1 else G[c, rows(s)]
            G[c, rows(s)] = jnp.where(flip(s, order(s)[i - 1]), X[i - 1, rows(s - n_raw)], mine)
        if i < bits:
            p_copy(s, i).start()

    def r_copy(s, i):
        b = order(s)[i]
        src = G.at[:, rows(s)] if i == 0 else F.at[:, rows(s)]
        return pltpu.make_async_remote_copy(
            src_ref=src,
            dst_ref=RX.at[i, :, rows(s)],
            send_sem=r_send.at[s, i],
            recv_sem=r_recv.at[s, i],
            device_id={"row": partner(b)},
            device_id_type=MESH,
        )

    def r_stage(s, i):
        if i == 0:
            G[c, rows(s)] = a_ref[rows(s)]
        if i > 0:
            copy = r_copy(s, i - 1)
            copy.wait_recv()
            copy.wait_send()
            flipped = flip(s, order(s)[i - 1])
            for k in range(n_col):
                mine = G[k, rows(s)] if i == 1 else F[k, rows(s)]
                F[k, rows(s)] = jnp.where(flipped, RX[i - 1, k, rows(s)], mine)
        if i < bits:
            r_copy(s, i).start()

    def pack():
        count = jnp.int32(0)
        place = [jnp.int32(0)] * CAP
        for j in range(width_tiles):
            flag = scr_ref[0, j]
            for i in range(CAP):
                here = flag * (count == i).astype(jnp.int32)
                place[i] = place[i] + here * (j + 1)
            count = count + flag
        at = lax.broadcasted_iota(jnp.int32, (16, TILE), 0) + 1
        for i in range(CAP):
            total = jnp.zeros((TILE, TILE), jnp.float32)
            for j in range(width_tiles):
                block = amp_ref[:, j * TILE:(j + 1) * TILE].astype(jnp.float32)
                total = jnp.where(place[i] == j + 1, block, total)
            AG[p, i * TILE:(i + 1) * TILE] = total.astype(jnp.bfloat16)
            mark = jnp.where(at == place[i], 1.0, 0.0)
            AG[p, CAP * TILE + i * 16:CAP * TILE + (i + 1) * 16] = mark.astype(jnp.bfloat16)

    def a_copy(b):
        size = 2**b
        block = pl.ds((p // size) * size, size)
        return pltpu.make_async_remote_copy(
            src_ref=AG.at[block],
            dst_ref=AG.at[block],
            send_sem=a_send.at[b],
            recv_sem=a_recv.at[b],
            device_id={"row": partner(b)},
            device_id_type=MESH,
        )

    def a_wait(b):
        size = 2**b
        other = pl.ds((partner(b) // size) * size, size)
        pltpu.make_async_remote_copy(
            src_ref=AG.at[other],
            dst_ref=AG.at[other],
            send_sem=a_send.at[b],
            recv_sem=a_recv.at[b],
            device_id={"row": partner(b)},
            device_id_type=MESH,
        ).wait_recv()

    def expand():
        def step(k, carry):
            first = AG[k, 0:TILE].astype(jnp.float32)
            second = AG[k, TILE:2 * TILE].astype(jnp.float32)
            marks = AG[k, 2 * TILE:2 * TILE + 32].astype(jnp.float32)
            at = pl.ds(pl.multiple_of(k * TILE, TILE), TILE)
            for j in range(width_tiles):
                value = first * marks[j:j + 1] + second * marks[16 + j:17 + j]
                W[at, j * TILE:(j + 1) * TILE] = value.astype(jnp.bfloat16)
            return carry

        lax.fori_loop(0, n_row, step, 0)

    depth = a_ref.shape[1]
    wide = 2 * TILE

    def o_copy(q):
        at = pl.ds(q * PAIR * TILE, PAIR * TILE)
        return pltpu.make_async_copy(O.at[at], out_ref.at[at], o_sem.at[q])

    def compute(q):
        at = pl.ds(q * PAIR * TILE, PAIR * TILE)
        held = F if q * PAIR < n_raw else G

        def step(n, carry):
            cols = pl.ds(pl.multiple_of(n * wide, wide), wide)
            total = jnp.zeros((PAIR * TILE, wide), jnp.float32)
            for k in range(n_col):
                total += jnp.dot(
                    held[k, at], W[k * depth:(k + 1) * depth, cols], preferred_element_type=jnp.float32
                )
            O[at, cols] = total.astype(jnp.bfloat16)
            return carry

        lax.fori_loop(0, amp_ref.shape[1] // wide, step, 0)
        o_copy(q).start()

    pairs = tiles // PAIR
    last = n_col - 1

    steps = []

    def at_place(place, step, *args):
        steps.append((place, len(steps), step, args))

    def own(s):
        if s >= n_raw:
            p_stage(s, bits)
        z_hop(s, 0)

    def a_stage(b):
        if b > 0:
            a_wait(b - 1)
        if b == 0:
            pack()
        if b < bits:
            a_copy(b).start()
        else:
            expand()

    shift = 0.6 * (bits - 3)
    for s in range(tiles):
        raw = s < n_raw
        late = 0.0 if raw else shift
        if raw:
            at_place(0.0, own, s)
        else:
            at_place((1.6 + 0.01 * (s - n_raw) if s < n_raw + PAIR else s - 1.5) + late, own, s)
            for i in range(bits):
                at_place(0.05 + 0.6 * i + 0.65 * (s // PAIR - 1), p_stage, s, i)
        for h in range(1, last):
            place = 0.6 * h + 0.4 * s if raw else s + 0.4 + 0.8 * (h - 1)
            at_place(place + late, z_hop, s, h)
        at_place((2.3 + 0.5 * s if raw else s + 2.2) + late, z_wait, s, last - 1)
        if raw:
            for i in range(bits + 1):
                at_place(2.85 + 1.7 * i - (0.9 if i == bits else 0.0), r_stage, s, i)
    for b in range(bits + 1):
        at_place(0.1 if b == 0 else 1.75 + 0.9 * (b - 1), a_stage, b)
    for q in range(pairs):
        if q * PAIR < n_raw:
            at_place(2.0 + 1.7 * bits, compute, q)
        else:
            at_place(q * PAIR + 3.25 + shift, compute, q)
    for place, index, step, args in sorted(steps, key=lambda entry: entry[:2]):
        step(*args)

    for s in range(tiles):
        for h in range(last):
            z_edges(s, h, lambda copy: copy.wait_send())
    for b in range(bits):
        a_copy(b).wait_send()
    for q in range(pairs):
        o_copy(q).wait()


def body(integrals, amplitudes, screen, next_owner):
    n_row, n_col = lax.axis_size("row"), lax.axis_size("col")
    bits = n_row.bit_length() - 1
    row_count, depth = integrals.shape
    width = amplitudes.shape[1]
    tiles = row_count // TILE
    n_raw = PAIR
    late = row_count - n_raw * TILE
    last = n_col - 1
    dma = pltpu.SemaphoreType.DMA
    vmem = pl.BlockSpec(memory_space=pltpu.VMEM)
    smem = pl.BlockSpec(memory_space=pltpu.SMEM)
    bf16 = jnp.bfloat16
    return pl.pallas_call(
        functools.partial(kernel, n_row, n_col, n_raw),
        out_shape=jax.ShapeDtypeStruct((row_count, width), bf16),
        in_specs=[vmem, vmem, smem, smem],
        out_specs=pl.BlockSpec(memory_space=pl.ANY),
        scratch_shapes=[
            pltpu.VMEM((n_col, row_count, depth), bf16),
            pltpu.VMEM((bits, late, depth), bf16),
            pltpu.VMEM((n_col, n_raw * TILE, depth), bf16),
            pltpu.VMEM((bits, n_col, n_raw * TILE, depth), bf16),
            pltpu.VMEM((n_row, CAP * TILE + 32, TILE), bf16),
            pltpu.VMEM((n_row * TILE, width), bf16),
            pltpu.VMEM((row_count, width), bf16),
            dma((tiles, last)),
            dma((tiles, last)),
            dma((tiles, last)),
            dma((tiles, last)),
            dma((tiles - n_raw, bits)),
            dma((tiles - n_raw, bits)),
            dma((n_raw, bits)),
            dma((n_raw, bits)),
            dma((bits,)),
            dma((bits,)),
            dma((tiles // PAIR,)),
        ],
        compiler_params=pltpu.CompilerParams(
            collective_id=0, has_side_effects=True, vmem_limit_bytes=56 * 1024 * 1024
        ),
    )(integrals, amplitudes, screen, next_owner)


def solution(mesh):
    placed = (P("row", "col"), P("row", "col"), P("row", "col"), P())
    return jax.shard_map(
        body, mesh=mesh, in_specs=placed, out_specs=P("row", "col"), check_vma=False
    )
```

```python
import functools

import jax
import jax.numpy as jnp
from jax import lax
from jax.experimental import pallas as pl
from jax.experimental.pallas import tpu as pltpu
from jax.sharding import PartitionSpec as P

TILE = 128
CAP = 2
PAIR = 2
MESH = pl.DeviceIdType.MESH


def kernel(
    n_row, n_col, n_raw,
    a_ref, amp_ref, scr_ref, own_ref, g_out, w_out,
    G, X, F, RX, AG, W,
    zr_send, zr_recv, zl_send, zl_recv, p_send, p_recv, r_send, r_recv, a_send, a_recv, g_sem, w_sem,
):
    p = lax.axis_index("row")
    c = lax.axis_index("col")
    bits = n_row.bit_length() - 1
    tiles = a_ref.shape[0] // TILE
    width_tiles = amp_ref.shape[1] // TILE

    def partner(b):
        mask = 2**b
        return p + mask - 2 * mask * ((p // mask) % 2)

    barrier = pltpu.get_barrier_semaphore()
    for b in range(bits):
        pl.semaphore_signal(barrier, inc=1, device_id={"row": partner(b)}, device_id_type=MESH)

    @pl.when(c > 0)
    def _():
        pl.semaphore_signal(barrier, inc=1, device_id={"col": c - 1}, device_id_type=MESH)

    @pl.when(c < n_col - 1)
    def _():
        pl.semaphore_signal(barrier, inc=1, device_id={"col": c + 1}, device_id_type=MESH)

    near = (c > 0).astype(jnp.int32) + (c < n_col - 1).astype(jnp.int32)
    pl.semaphore_wait(barrier, bits + near)

    def rows(s):
        return pl.ds(s * TILE, TILE)

    def z_copy(s, h, right, block):
        src = a_ref.at[rows(s)] if h == 0 and s < n_raw else G.at[block, rows(s)]
        send, recv = (zr_send, zr_recv) if right else (zl_send, zl_recv)
        return pltpu.make_async_remote_copy(
            src_ref=src,
            dst_ref=G.at[block, rows(s)],
            send_sem=send.at[s, h],
            recv_sem=recv.at[s, h],
            device_id={"col": c + 1 if right else c - 1},
            device_id_type=MESH,
        )

    def z_wait(s, h):
        @pl.when(c - 1 - h >= 0)
        def _():
            z_copy(s, h, True, c - 1 - h).wait_recv()

        @pl.when(c + 1 + h < n_col)
        def _():
            z_copy(s, h, False, c + 1 + h).wait_recv()

    def z_edges(s, h, act):
        @pl.when((c - h >= 0) & (c < n_col - 1))
        def _():
            act(z_copy(s, h, True, c - h))

        @pl.when((c + h < n_col) & (c > 0))
        def _():
            act(z_copy(s, h, False, c + h))

    def z_hop(s, h):
        if h > 0:
            z_wait(s, h - 1)
        z_edges(s, h, lambda copy: copy.start())

    def order(s):
        far = list(range(1, bits))
        turn = s % len(far)
        return far[turn:] + far[:turn] + [0]

    def flip(s, b):
        return (own_ref[s] // 2**b) % 2 == 1

    def p_copy(s, i):
        b = order(s)[i]
        src = a_ref.at[rows(s)] if i == 0 else G.at[c, rows(s)]
        return pltpu.make_async_remote_copy(
            src_ref=src,
            dst_ref=X.at[i, rows(s - n_raw)],
            send_sem=p_send.at[s - n_raw, i],
            recv_sem=p_recv.at[s - n_raw, i],
            device_id={"row": partner(b)},
            device_id_type=MESH,
        )

    def p_stage(s, i):
        if i > 0:
            copy = p_copy(s, i - 1)
            copy.wait_recv()
            copy.wait_send()
            mine = a_ref[rows(s)] if i == 1 else G[c, rows(s)]
            G[c, rows(s)] = jnp.where(flip(s, order(s)[i - 1]), X[i - 1, rows(s - n_raw)], mine)
        if i < bits:
            p_copy(s, i).start()

    def r_copy(s, i):
        b = order(s)[i]
        src = G.at[:, rows(s)] if i == 0 else F.at[:, rows(s)]
        return pltpu.make_async_remote_copy(
            src_ref=src,
            dst_ref=RX.at[i, :, rows(s)],
            send_sem=r_send.at[s, i],
            recv_sem=r_recv.at[s, i],
            device_id={"row": partner(b)},
            device_id_type=MESH,
        )

    def r_stage(s, i):
        if i == 0:
            G[c, rows(s)] = a_ref[rows(s)]
        if i > 0:
            copy = r_copy(s, i - 1)
            copy.wait_recv()
            copy.wait_send()
            flipped = flip(s, order(s)[i - 1])
            for k in range(n_col):
                mine = G[k, rows(s)] if i == 1 else F[k, rows(s)]
                F[k, rows(s)] = jnp.where(flipped, RX[i - 1, k, rows(s)], mine)
        if i < bits:
            r_copy(s, i).start()

    def pack():
        count = jnp.int32(0)
        place = [jnp.int32(0)] * CAP
        for j in range(width_tiles):
            flag = scr_ref[0, j]
            for i in range(CAP):
                here = flag * (count == i).astype(jnp.int32)
                place[i] = place[i] + here * (j + 1)
            count = count + flag
        at = lax.broadcasted_iota(jnp.int32, (16, TILE), 0) + 1
        for i in range(CAP):
            total = jnp.zeros((TILE, TILE), jnp.float32)
            for j in range(width_tiles):
                block = amp_ref[:, j * TILE:(j + 1) * TILE].astype(jnp.float32)
                total = jnp.where(place[i] == j + 1, block, total)
            AG[p, i * TILE:(i + 1) * TILE] = total.astype(jnp.bfloat16)
            mark = jnp.where(at == place[i], 1.0, 0.0)
            AG[p, CAP * TILE + i * 16:CAP * TILE + (i + 1) * 16] = mark.astype(jnp.bfloat16)

    def a_copy(b):
        size = 2**b
        block = pl.ds((p // size) * size, size)
        return pltpu.make_async_remote_copy(
            src_ref=AG.at[block],
            dst_ref=AG.at[block],
            send_sem=a_send.at[b],
            recv_sem=a_recv.at[b],
            device_id={"row": partner(b)},
            device_id_type=MESH,
        )

    def a_wait(b):
        size = 2**b
        other = pl.ds((partner(b) // size) * size, size)
        pltpu.make_async_remote_copy(
            src_ref=AG.at[other],
            dst_ref=AG.at[other],
            send_sem=a_send.at[b],
            recv_sem=a_recv.at[b],
            device_id={"row": partner(b)},
            device_id_type=MESH,
        ).wait_recv()

    def expand():
        def step(k, carry):
            first = AG[k, 0:TILE].astype(jnp.float32)
            second = AG[k, TILE:2 * TILE].astype(jnp.float32)
            marks = AG[k, 2 * TILE:2 * TILE + 32].astype(jnp.float32)
            at = pl.ds(pl.multiple_of(k * TILE, TILE), TILE)
            for j in range(width_tiles):
                value = first * marks[j:j + 1] + second * marks[16 + j:17 + j]
                W[at, j * TILE:(j + 1) * TILE] = value.astype(jnp.bfloat16)
            return carry

        lax.fori_loop(0, n_row, step, 0)

    depth = a_ref.shape[1]

    def g_copy(s, k):
        held = F if s < n_raw else G
        return pltpu.make_async_copy(
            held.at[k, rows(s)], g_out.at[rows(s), pl.ds(k * depth, depth)], g_sem.at[s, k]
        )

    def put(s):
        for k in range(n_col):
            g_copy(s, k).start()

    w_copy = pltpu.make_async_copy(W, w_out, w_sem.at[0])

    last = n_col - 1

    steps = []

    def at_place(place, step, *args):
        steps.append((place, len(steps), step, args))

    def own(s):
        if s >= n_raw:
            p_stage(s, bits)
        z_hop(s, 0)

    def a_stage(b):
        if b > 0:
            a_wait(b - 1)
        if b == 0:
            pack()
        if b < bits:
            a_copy(b).start()
        else:
            expand()
            w_copy.start()

    shift = 0.6 * (bits - 3)
    for s in range(tiles):
        raw = s < n_raw
        late = 0.0 if raw else shift
        if raw:
            at_place(0.0, own, s)
        else:
            at_place((1.6 + 0.01 * (s - n_raw) if s < n_raw + PAIR else s - 1.5) + late, own, s)
            for i in range(bits):
                at_place(0.05 + 0.6 * i + 0.65 * (s // PAIR - 1), p_stage, s, i)
        for h in range(1, last):
            place = 0.6 * h + 0.4 * s if raw else s + 0.4 + 0.8 * (h - 1)
            at_place(place + late, z_hop, s, h)
        at_place((2.3 + 0.5 * s if raw else s + 2.2) + late, z_wait, s, last - 1)
        at_place((2.0 + 1.7 * bits if raw else s + 2.2) + late, put, s)
        if raw:
            for i in range(bits + 1):
                at_place(2.85 + 1.7 * i - (0.9 if i == bits else 0.0), r_stage, s, i)
    for b in range(bits + 1):
        at_place(0.1 if b == 0 else 1.75 + 0.9 * (b - 1), a_stage, b)
    for place, index, step, args in sorted(steps, key=lambda entry: entry[:2]):
        step(*args)

    for s in range(tiles):
        for h in range(last):
            z_edges(s, h, lambda copy: copy.wait_send())
    for b in range(bits):
        a_copy(b).wait_send()
    for s in range(tiles):
        for k in range(n_col):
            g_copy(s, k).wait()
    w_copy.wait()


def body(integrals, amplitudes, screen, next_owner):
    n_row, n_col = lax.axis_size("row"), lax.axis_size("col")
    bits = n_row.bit_length() - 1
    row_count, depth = integrals.shape
    width = amplitudes.shape[1]
    tiles = row_count // TILE
    n_raw = PAIR
    late = row_count - n_raw * TILE
    last = n_col - 1
    dma = pltpu.SemaphoreType.DMA
    vmem = pl.BlockSpec(memory_space=pltpu.VMEM)
    smem = pl.BlockSpec(memory_space=pltpu.SMEM)
    bf16 = jnp.bfloat16
    gathered, screened = pl.pallas_call(
        functools.partial(kernel, n_row, n_col, n_raw),
        out_shape=[
            jax.ShapeDtypeStruct((row_count, n_col * depth), bf16),
            jax.ShapeDtypeStruct((n_row * TILE, width), bf16),
        ],
        in_specs=[vmem, vmem, smem, smem],
        out_specs=[pl.BlockSpec(memory_space=pl.ANY)] * 2,
        scratch_shapes=[
            pltpu.VMEM((n_col, row_count, depth), bf16),
            pltpu.VMEM((bits, late, depth), bf16),
            pltpu.VMEM((n_col, n_raw * TILE, depth), bf16),
            pltpu.VMEM((bits, n_col, n_raw * TILE, depth), bf16),
            pltpu.VMEM((n_row, CAP * TILE + 32, TILE), bf16),
            pltpu.VMEM((n_row * TILE, width), bf16),
            dma((tiles, last)),
            dma((tiles, last)),
            dma((tiles, last)),
            dma((tiles, last)),
            dma((tiles - n_raw, bits)),
            dma((tiles - n_raw, bits)),
            dma((n_raw, bits)),
            dma((n_raw, bits)),
            dma((bits,)),
            dma((bits,)),
            dma((tiles, n_col)),
            dma((1,)),
        ],
        compiler_params=pltpu.CompilerParams(
            collective_id=0, has_side_effects=True, vmem_limit_bytes=56 * 1024 * 1024
        ),
    )(integrals, amplitudes, screen, next_owner)
    return jnp.dot(gathered, screened, preferred_element_type=jnp.float32).astype(bf16)


def solution(mesh):
    placed = (P("row", "col"), P("row", "col"), P("row", "col"), P())
    return jax.shard_map(
        body, mesh=mesh, in_specs=placed, out_specs=P("row", "col"), check_vma=False
    )
```

```python
import functools

import jax
import jax.numpy as jnp
from jax import lax
from jax.experimental import pallas as pl
from jax.experimental.pallas import tpu as pltpu
from jax.sharding import PartitionSpec as P

TILE = 128
CAP = 2
PAIR = 2
LEAD = 2
MESH = pl.DeviceIdType.MESH


def kernel(
    n_row, n_col, n_raw,
    a_ref, amp_ref, scr_ref, own_ref, g_out, w_out,
    G, X, F, RX, AG, W,
    zr_send, zr_recv, zl_send, zl_recv, p_send, p_recv, r_send, r_recv, a_send, a_recv, g_sem, w_sem,
):
    p = lax.axis_index("row")
    c = lax.axis_index("col")
    bits = n_row.bit_length() - 1
    tiles = a_ref.shape[0] // TILE
    width_tiles = amp_ref.shape[1] // TILE

    def partner(b):
        mask = 2**b
        return p + mask - 2 * mask * ((p // mask) % 2)

    barrier = pltpu.get_barrier_semaphore()
    for b in range(bits):
        pl.semaphore_signal(barrier, inc=1, device_id={"row": partner(b)}, device_id_type=MESH)

    @pl.when(c > 0)
    def _():
        pl.semaphore_signal(barrier, inc=1, device_id={"col": c - 1}, device_id_type=MESH)

    @pl.when(c < n_col - 1)
    def _():
        pl.semaphore_signal(barrier, inc=1, device_id={"col": c + 1}, device_id_type=MESH)

    near = (c > 0).astype(jnp.int32) + (c < n_col - 1).astype(jnp.int32)
    pl.semaphore_wait(barrier, bits + near)

    def rows(s):
        return pl.ds(s * TILE, TILE)

    def z_copy(s, h, right, block):
        src = a_ref.at[rows(s)] if h == 0 and s < n_raw else G.at[block, rows(s)]
        send, recv = (zr_send, zr_recv) if right else (zl_send, zl_recv)
        return pltpu.make_async_remote_copy(
            src_ref=src,
            dst_ref=G.at[block, rows(s)],
            send_sem=send.at[s, h],
            recv_sem=recv.at[s, h],
            device_id={"col": c + 1 if right else c - 1},
            device_id_type=MESH,
        )

    def z_wait(s, h):
        @pl.when(c - 1 - h >= 0)
        def _():
            z_copy(s, h, True, c - 1 - h).wait_recv()

        @pl.when(c + 1 + h < n_col)
        def _():
            z_copy(s, h, False, c + 1 + h).wait_recv()

    def z_edges(s, h, act):
        @pl.when((c - h >= 0) & (c < n_col - 1))
        def _():
            act(z_copy(s, h, True, c - h))

        @pl.when((c + h < n_col) & (c > 0))
        def _():
            act(z_copy(s, h, False, c + h))

    def z_hop(s, h):
        if h > 0:
            z_wait(s, h - 1)
        z_edges(s, h, lambda copy: copy.start())

    def order(s):
        far = list(range(1, bits))
        turn = s % len(far)
        return far[turn:] + far[:turn] + [0]

    def flip(s, b):
        return (own_ref[s] // 2**b) % 2 == 1

    def p_copy(s, i):
        b = order(s)[i]
        src = a_ref.at[rows(s)] if i == 0 else G.at[c, rows(s)]
        return pltpu.make_async_remote_copy(
            src_ref=src,
            dst_ref=X.at[i, rows(s - n_raw)],
            send_sem=p_send.at[s - n_raw, i],
            recv_sem=p_recv.at[s - n_raw, i],
            device_id={"row": partner(b)},
            device_id_type=MESH,
        )

    def p_stage(s, i):
        if i > 0:
            copy = p_copy(s, i - 1)
            copy.wait_recv()
            copy.wait_send()
            mine = a_ref[rows(s)] if i == 1 else G[c, rows(s)]
            G[c, rows(s)] = jnp.where(flip(s, order(s)[i - 1]), X[i - 1, rows(s - n_raw)], mine)
        if i < bits:
            p_copy(s, i).start()

    def r_copy(s, i):
        b = order(s)[i]
        src = G.at[:, rows(s)] if i == 0 else F.at[:, rows(s)]
        return pltpu.make_async_remote_copy(
            src_ref=src,
            dst_ref=RX.at[i, :, rows(s)],
            send_sem=r_send.at[s, i],
            recv_sem=r_recv.at[s, i],
            device_id={"row": partner(b)},
            device_id_type=MESH,
        )

    def r_stage(s, i):
        if i == 0:
            G[c, rows(s)] = a_ref[rows(s)]
        if i > 0:
            copy = r_copy(s, i - 1)
            copy.wait_recv()
            copy.wait_send()
            flipped = flip(s, order(s)[i - 1])
            for k in range(n_col):
                mine = G[k, rows(s)] if i == 1 else F[k, rows(s)]
                F[k, rows(s)] = jnp.where(flipped, RX[i - 1, k, rows(s)], mine)
        if i < bits:
            r_copy(s, i).start()

    def pack():
        count = jnp.int32(0)
        place = [jnp.int32(0)] * CAP
        for j in range(width_tiles):
            flag = scr_ref[0, j]
            for i in range(CAP):
                here = flag * (count == i).astype(jnp.int32)
                place[i] = place[i] + here * (j + 1)
            count = count + flag
        at = lax.broadcasted_iota(jnp.int32, (16, TILE), 0) + 1
        for i in range(CAP):
            total = jnp.zeros((TILE, TILE), jnp.float32)
            for j in range(width_tiles):
                block = amp_ref[:, j * TILE:(j + 1) * TILE].astype(jnp.float32)
                total = jnp.where(place[i] == j + 1, block, total)
            AG[p, i * TILE:(i + 1) * TILE] = total.astype(jnp.bfloat16)
            mark = jnp.where(at == place[i], 1.0, 0.0)
            AG[p, CAP * TILE + i * 16:CAP * TILE + (i + 1) * 16] = mark.astype(jnp.bfloat16)

    def a_copy(b):
        size = 2**b
        block = pl.ds((p // size) * size, size)
        return pltpu.make_async_remote_copy(
            src_ref=AG.at[block],
            dst_ref=AG.at[block],
            send_sem=a_send.at[b],
            recv_sem=a_recv.at[b],
            device_id={"row": partner(b)},
            device_id_type=MESH,
        )

    def a_wait(b):
        size = 2**b
        other = pl.ds((partner(b) // size) * size, size)
        pltpu.make_async_remote_copy(
            src_ref=AG.at[other],
            dst_ref=AG.at[other],
            send_sem=a_send.at[b],
            recv_sem=a_recv.at[b],
            device_id={"row": partner(b)},
            device_id_type=MESH,
        ).wait_recv()

    def expand():
        def step(k, carry):
            first = AG[k, 0:TILE].astype(jnp.float32)
            second = AG[k, TILE:2 * TILE].astype(jnp.float32)
            marks = AG[k, 2 * TILE:2 * TILE + 32].astype(jnp.float32)
            at = pl.ds(pl.multiple_of(k * TILE, TILE), TILE)
            for j in range(width_tiles):
                value = first * marks[j:j + 1] + second * marks[16 + j:17 + j]
                W[at, j * TILE:(j + 1) * TILE] = value.astype(jnp.bfloat16)
            return carry

        lax.fori_loop(0, n_row, step, 0)

    depth = a_ref.shape[1]

    def g_copy(s, k):
        held = F if s < n_raw else G
        return pltpu.make_async_copy(
            held.at[k, rows(s)], g_out.at[rows(s), pl.ds(k * depth, depth)], g_sem.at[s, k]
        )

    def put(s):
        for k in range(n_col):
            g_copy(s, k).start()

    w_copy = pltpu.make_async_copy(W, w_out, w_sem.at[0])

    last = n_col - 1

    steps = []

    def at_place(place, step, *args):
        steps.append((place, len(steps), step, args))

    def own(s):
        if s >= n_raw:
            p_stage(s, bits)
        z_hop(s, 0)

    def a_stage(b):
        if b > 0:
            a_wait(b - 1)
        if b == 0:
            pack()
        if b < bits:
            a_copy(b).start()
        else:
            expand()
            w_copy.start()

    shift = 0.6 * (bits - 3)
    for s in range(tiles):
        raw = s < n_raw
        late = 0.0 if raw else shift
        if raw:
            at_place(0.0, own, s)
        else:
            v = s - n_raw + LEAD
            at_place((1.6 + 0.01 * (s - n_raw) if v < 2 * LEAD else v - 1.5) + late, own, s)
            for i in range(bits):
                at_place(0.05 + 0.6 * i + 0.65 * ((s - n_raw) // PAIR), p_stage, s, i)
        for h in range(1, last):
            place = 0.6 * h + 0.4 * s if raw else v + 0.4 + 0.8 * (h - 1)
            at_place(place + late, z_hop, s, h)
        at_place((2.3 + 0.5 * s if raw else v + 2.2) + late, z_wait, s, last - 1)
        at_place((2.0 + 1.7 * bits if raw else v + 2.2) + late, put, s)
        if raw:
            for i in range(bits + 1):
                at_place(2.85 + 1.7 * i - (0.9 if i == bits else 0.0), r_stage, s, i)
    for b in range(bits + 1):
        at_place(0.1 if b == 0 else 1.75 + 0.9 * (b - 1), a_stage, b)
    for place, index, step, args in sorted(steps, key=lambda entry: entry[:2]):
        step(*args)

    for s in range(tiles):
        for h in range(last):
            z_edges(s, h, lambda copy: copy.wait_send())
    for b in range(bits):
        a_copy(b).wait_send()
    for s in range(tiles):
        for k in range(n_col):
            g_copy(s, k).wait()
    w_copy.wait()


def body(integrals, amplitudes, screen, next_owner):
    n_row, n_col = lax.axis_size("row"), lax.axis_size("col")
    bits = n_row.bit_length() - 1
    row_count, depth = integrals.shape
    width = amplitudes.shape[1]
    tiles = row_count // TILE
    n_raw = 0
    late = row_count - n_raw * TILE
    last = n_col - 1
    dma = pltpu.SemaphoreType.DMA
    vmem = pl.BlockSpec(memory_space=pltpu.VMEM)
    smem = pl.BlockSpec(memory_space=pltpu.SMEM)
    bf16 = jnp.bfloat16
    gathered, screened = pl.pallas_call(
        functools.partial(kernel, n_row, n_col, n_raw),
        out_shape=[
            jax.ShapeDtypeStruct((row_count, n_col * depth), bf16),
            jax.ShapeDtypeStruct((n_row * TILE, width), bf16),
        ],
        in_specs=[vmem, vmem, smem, smem],
        out_specs=[pl.BlockSpec(memory_space=pl.ANY)] * 2,
        scratch_shapes=[
            pltpu.VMEM((n_col, row_count, depth), bf16),
            pltpu.VMEM((bits, late, depth), bf16),
            pltpu.VMEM((n_col, max(n_raw, 1) * TILE, depth), bf16),
            pltpu.VMEM((bits, n_col, max(n_raw, 1) * TILE, depth), bf16),
            pltpu.VMEM((n_row, CAP * TILE + 32, TILE), bf16),
            pltpu.VMEM((n_row * TILE, width), bf16),
            dma((tiles, last)),
            dma((tiles, last)),
            dma((tiles, last)),
            dma((tiles, last)),
            dma((tiles - n_raw, bits)),
            dma((tiles - n_raw, bits)),
            dma((max(n_raw, 1), bits)),
            dma((max(n_raw, 1), bits)),
            dma((bits,)),
            dma((bits,)),
            dma((tiles, n_col)),
            dma((1,)),
        ],
        compiler_params=pltpu.CompilerParams(
            collective_id=0, has_side_effects=True, vmem_limit_bytes=56 * 1024 * 1024
        ),
    )(integrals, amplitudes, screen, next_owner)
    return jnp.dot(gathered, screened, preferred_element_type=jnp.float32).astype(bf16)


def solution(mesh):
    placed = (P("row", "col"), P("row", "col"), P("row", "col"), P())
    return jax.shard_map(
        body, mesh=mesh, in_specs=placed, out_specs=P("row", "col"), check_vma=False
    )
```

```python
import functools

import jax
import jax.numpy as jnp
from jax import lax
from jax.experimental import pallas as pl
from jax.experimental.pallas import tpu as pltpu
from jax.sharding import PartitionSpec as P

TILE = 128
CAP = 2
PAIR = 2
MESH = pl.DeviceIdType.MESH


def kernel(
    n_row, n_col, n_raw,
    a_ref, amp_ref, scr_ref, own_ref, g_out, w_out,
    G, X, F, RX, AG, W,
    zr_send, zr_recv, zl_send, zl_recv, p_send, p_recv, r_send, r_recv, a_send, a_recv, g_sem, w_sem,
):
    p = lax.axis_index("row")
    c = lax.axis_index("col")
    bits = n_row.bit_length() - 1
    tiles = a_ref.shape[0] // TILE
    width_tiles = amp_ref.shape[1] // TILE

    def partner(b):
        mask = 2**b
        return p + mask - 2 * mask * ((p // mask) % 2)

    barrier = pltpu.get_barrier_semaphore()
    for b in range(bits):
        pl.semaphore_signal(barrier, inc=1, device_id={"row": partner(b)}, device_id_type=MESH)

    @pl.when(c > 0)
    def _():
        pl.semaphore_signal(barrier, inc=1, device_id={"col": c - 1}, device_id_type=MESH)

    @pl.when(c < n_col - 1)
    def _():
        pl.semaphore_signal(barrier, inc=1, device_id={"col": c + 1}, device_id_type=MESH)

    near = (c > 0).astype(jnp.int32) + (c < n_col - 1).astype(jnp.int32)
    pl.semaphore_wait(barrier, bits + near)

    def rows(s):
        return pl.ds(s * TILE, TILE)

    def z_copy(q, h, right, block):
        at = pl.ds(q * PAIR * TILE, PAIR * TILE)
        src = a_ref.at[at] if h == 0 and q * PAIR < n_raw else G.at[block, at]
        send, recv = (zr_send, zr_recv) if right else (zl_send, zl_recv)
        return pltpu.make_async_remote_copy(
            src_ref=src,
            dst_ref=G.at[block, at],
            send_sem=send.at[q, h],
            recv_sem=recv.at[q, h],
            device_id={"col": c + 1 if right else c - 1},
            device_id_type=MESH,
        )

    def z_wait(q, h):
        @pl.when(c - 1 - h >= 0)
        def _():
            z_copy(q, h, True, c - 1 - h).wait_recv()

        @pl.when(c + 1 + h < n_col)
        def _():
            z_copy(q, h, False, c + 1 + h).wait_recv()

    def z_edges(q, h, act):
        @pl.when((c - h >= 0) & (c < n_col - 1))
        def _():
            act(z_copy(q, h, True, c - h))

        @pl.when((c + h < n_col) & (c > 0))
        def _():
            act(z_copy(q, h, False, c + h))

    def z_hop(q, h):
        if h > 0:
            z_wait(q, h - 1)
        z_edges(q, h, lambda copy: copy.start())

    def order(s):
        far = list(range(1, bits))
        turn = s % len(far)
        return far[turn:] + far[:turn] + [0]

    def flip(s, b):
        return (own_ref[s] // 2**b) % 2 == 1

    def p_copy(s, i):
        b = order(s)[i]
        src = a_ref.at[rows(s)] if i == 0 else G.at[c, rows(s)]
        return pltpu.make_async_remote_copy(
            src_ref=src,
            dst_ref=X.at[i, rows(s - n_raw)],
            send_sem=p_send.at[s - n_raw, i],
            recv_sem=p_recv.at[s - n_raw, i],
            device_id={"row": partner(b)},
            device_id_type=MESH,
        )

    def p_stage(s, i):
        if i > 0:
            copy = p_copy(s, i - 1)
            copy.wait_recv()
            copy.wait_send()
            mine = a_ref[rows(s)] if i == 1 else G[c, rows(s)]
            G[c, rows(s)] = jnp.where(flip(s, order(s)[i - 1]), X[i - 1, rows(s - n_raw)], mine)
        if i < bits:
            p_copy(s, i).start()

    def r_copy(s, i):
        b = order(s)[i]
        src = G.at[:, rows(s)] if i == 0 else F.at[:, rows(s)]
        return pltpu.make_async_remote_copy(
            src_ref=src,
            dst_ref=RX.at[i, :, rows(s)],
            send_sem=r_send.at[s, i],
            recv_sem=r_recv.at[s, i],
            device_id={"row": partner(b)},
            device_id_type=MESH,
        )

    def r_stage(s, i):
        if i == 0:
            G[c, rows(s)] = a_ref[rows(s)]
        if i > 0:
            copy = r_copy(s, i - 1)
            copy.wait_recv()
            copy.wait_send()
            flipped = flip(s, order(s)[i - 1])
            for k in range(n_col):
                mine = G[k, rows(s)] if i == 1 else F[k, rows(s)]
                F[k, rows(s)] = jnp.where(flipped, RX[i - 1, k, rows(s)], mine)
        if i < bits:
            r_copy(s, i).start()

    def pack():
        count = jnp.int32(0)
        place = [jnp.int32(0)] * CAP
        for j in range(width_tiles):
            flag = scr_ref[0, j]
            for i in range(CAP):
                here = flag * (count == i).astype(jnp.int32)
                place[i] = place[i] + here * (j + 1)
            count = count + flag
        at = lax.broadcasted_iota(jnp.int32, (16, TILE), 0) + 1
        for i in range(CAP):
            total = jnp.zeros((TILE, TILE), jnp.float32)
            for j in range(width_tiles):
                block = amp_ref[:, j * TILE:(j + 1) * TILE].astype(jnp.float32)
                total = jnp.where(place[i] == j + 1, block, total)
            AG[p, i * TILE:(i + 1) * TILE] = total.astype(jnp.bfloat16)
            mark = jnp.where(at == place[i], 1.0, 0.0)
            AG[p, CAP * TILE + i * 16:CAP * TILE + (i + 1) * 16] = mark.astype(jnp.bfloat16)

    def a_copy(b):
        size = 2**b
        block = pl.ds((p // size) * size, size)
        return pltpu.make_async_remote_copy(
            src_ref=AG.at[block],
            dst_ref=AG.at[block],
            send_sem=a_send.at[b],
            recv_sem=a_recv.at[b],
            device_id={"row": partner(b)},
            device_id_type=MESH,
        )

    def a_wait(b):
        size = 2**b
        other = pl.ds((partner(b) // size) * size, size)
        pltpu.make_async_remote_copy(
            src_ref=AG.at[other],
            dst_ref=AG.at[other],
            send_sem=a_send.at[b],
            recv_sem=a_recv.at[b],
            device_id={"row": partner(b)},
            device_id_type=MESH,
        ).wait_recv()

    def expand():
        def step(k, carry):
            first = AG[k, 0:TILE].astype(jnp.float32)
            second = AG[k, TILE:2 * TILE].astype(jnp.float32)
            marks = AG[k, 2 * TILE:2 * TILE + 32].astype(jnp.float32)
            at = pl.ds(pl.multiple_of(k * TILE, TILE), TILE)
            for j in range(width_tiles):
                value = first * marks[j:j + 1] + second * marks[16 + j:17 + j]
                W[at, j * TILE:(j + 1) * TILE] = value.astype(jnp.bfloat16)
            return carry

        lax.fori_loop(0, n_row, step, 0)

    depth = a_ref.shape[1]

    def g_copy(s, k):
        held = F if s < n_raw else G
        return pltpu.make_async_copy(
            held.at[k, rows(s)], g_out.at[rows(s), pl.ds(k * depth, depth)], g_sem.at[s, k]
        )

    def put(s):
        for k in range(n_col):
            g_copy(s, k).start()

    w_copy = pltpu.make_async_copy(W, w_out, w_sem.at[0])

    last = n_col - 1
    pairs, raw_pairs = tiles // PAIR, n_raw // PAIR

    def pair(q):
        return range(q * PAIR, (q + 1) * PAIR)

    steps = []

    def at_place(place, step, *args):
        steps.append((place, len(steps), step, args))

    def a_stage(b):
        if b > 0:
            a_wait(b - 1)
        if b == 0:
            pack()
        if b < bits:
            a_copy(b).start()
        else:
            expand()
            w_copy.start()

    def own(q):
        if q >= raw_pairs:
            for s in pair(q):
                p_stage(s, bits)
        z_hop(q, 0)

    def put_pair(q):
        for s in pair(q):
            put(s)

    shift = 0.6 * (bits - 3)
    for q in range(pairs):
        j = q - raw_pairs
        if q < raw_pairs:
            at_place(0.0, own, q)
            at_place(2.6, z_wait, q, last - 1)
            at_place(2.2 + 1.7 * bits, put_pair, q)
        else:
            at_place((1.6 if j == 0 else 1.0 + 1.2 * j) + shift, own, q)
            at_place(4.4 + 1.5 * j + shift, z_wait, q, last - 1)
            at_place(4.4 + 1.5 * j + shift, put_pair, q)
        for h in range(1, last):
            if q < raw_pairs:
                at_place(0.75 + 0.95 * (h - 1), z_hop, q, h)
            else:
                at_place(2.7 + 1.3 * j + (0.9 + 0.2 * j) * (h - 1) + shift, z_hop, q, h)
        for s in pair(q):
            for i in range(bits + 1):
                if q < raw_pairs:
                    at_place(2.65 + 1.7 * i - (0.9 if i == bits else 0.0), r_stage, s, i)
                elif i < bits:
                    at_place(0.05 + 0.6 * i + 0.65 * j, p_stage, s, i)
    for b in range(bits + 1):
        at_place(0.1 if b == 0 else 1.75 + 0.9 * (b - 1), a_stage, b)
    for place, index, step, args in sorted(steps, key=lambda entry: entry[:2]):
        step(*args)

    for q in range(pairs):
        for h in range(last):
            z_edges(q, h, lambda copy: copy.wait_send())
    for b in range(bits):
        a_copy(b).wait_send()
    for s in range(tiles):
        for k in range(n_col):
            g_copy(s, k).wait()
    w_copy.wait()


def multiply(left_ref, right_ref, out_ref):
    total = jnp.dot(left_ref[...], right_ref[...], preferred_element_type=jnp.float32)
    out_ref[...] = total.astype(out_ref.dtype)


def body(integrals, amplitudes, screen, next_owner):
    n_row, n_col = lax.axis_size("row"), lax.axis_size("col")
    bits = n_row.bit_length() - 1
    row_count, depth = integrals.shape
    width = amplitudes.shape[1]
    tiles = row_count // TILE
    n_raw = PAIR
    late = row_count - n_raw * TILE
    last = n_col - 1
    dma = pltpu.SemaphoreType.DMA
    vmem = pl.BlockSpec(memory_space=pltpu.VMEM)
    smem = pl.BlockSpec(memory_space=pltpu.SMEM)
    bf16 = jnp.bfloat16
    gathered, screened = pl.pallas_call(
        functools.partial(kernel, n_row, n_col, n_raw),
        out_shape=[
            jax.ShapeDtypeStruct((row_count, n_col * depth), bf16),
            jax.ShapeDtypeStruct((n_row * TILE, width), bf16),
        ],
        in_specs=[vmem, vmem, smem, smem],
        out_specs=[pl.BlockSpec(memory_space=pl.ANY)] * 2,
        scratch_shapes=[
            pltpu.VMEM((n_col, row_count, depth), bf16),
            pltpu.VMEM((bits, late, depth), bf16),
            pltpu.VMEM((n_col, n_raw * TILE, depth), bf16),
            pltpu.VMEM((bits, n_col, n_raw * TILE, depth), bf16),
            pltpu.VMEM((n_row, CAP * TILE + 32, TILE), bf16),
            pltpu.VMEM((n_row * TILE, width), bf16),
            dma((tiles // PAIR, last)),
            dma((tiles // PAIR, last)),
            dma((tiles // PAIR, last)),
            dma((tiles // PAIR, last)),
            dma((tiles - n_raw, bits)),
            dma((tiles - n_raw, bits)),
            dma((n_raw, bits)),
            dma((n_raw, bits)),
            dma((bits,)),
            dma((bits,)),
            dma((tiles, n_col)),
            dma((1,)),
        ],
        compiler_params=pltpu.CompilerParams(
            collective_id=0, has_side_effects=True, vmem_limit_bytes=56 * 1024 * 1024
        ),
    )(integrals, amplitudes, screen, next_owner)
    wide = 2 * TILE
    return pl.pallas_call(
        multiply,
        out_shape=jax.ShapeDtypeStruct((row_count, width), bf16),
        grid=(width // wide,),
        in_specs=[
            pl.BlockSpec(gathered.shape, lambda n: (0, 0)),
            pl.BlockSpec((screened.shape[0], wide), lambda n: (0, n)),
        ],
        out_specs=pl.BlockSpec((row_count, wide), lambda n: (0, n)),
        compiler_params=pltpu.CompilerParams(vmem_limit_bytes=48 * 1024 * 1024),
    )(gathered, screened)


def solution(mesh):
    placed = (P("row", "col"), P("row", "col"), P("row", "col"), P())
    return jax.shard_map(
        body, mesh=mesh, in_specs=placed, out_specs=P("row", "col"), check_vma=False
    )
```

```python
import functools

import jax
import jax.numpy as jnp
from jax import lax
from jax.experimental import pallas as pl
from jax.experimental.pallas import tpu as pltpu
from jax.sharding import PartitionSpec as P

TILE = 128
CAP = 2
PAIR = 2
MESH = pl.DeviceIdType.MESH


def kernel(
    n_row, n_col, n_raw,
    a_ref, amp_ref, scr_ref, own_ref, g_out, w_out, part_out,
    G, X, F, RX, AG, W, O,
    zr_send, zr_recv, zl_send, zl_recv, p_send, p_recv, r_send, r_recv, a_send, a_recv, g_sem, w_sem, o_sem,
):
    p = lax.axis_index("row")
    c = lax.axis_index("col")
    bits = n_row.bit_length() - 1
    tiles = a_ref.shape[0] // TILE
    width_tiles = amp_ref.shape[1] // TILE

    def partner(b):
        mask = 2**b
        return p + mask - 2 * mask * ((p // mask) % 2)

    barrier = pltpu.get_barrier_semaphore()
    for b in range(bits):
        pl.semaphore_signal(barrier, inc=1, device_id={"row": partner(b)}, device_id_type=MESH)

    @pl.when(c > 0)
    def _():
        pl.semaphore_signal(barrier, inc=1, device_id={"col": c - 1}, device_id_type=MESH)

    @pl.when(c < n_col - 1)
    def _():
        pl.semaphore_signal(barrier, inc=1, device_id={"col": c + 1}, device_id_type=MESH)

    near = (c > 0).astype(jnp.int32) + (c < n_col - 1).astype(jnp.int32)
    pl.semaphore_wait(barrier, bits + near)

    def rows(s):
        return pl.ds(s * TILE, TILE)

    def z_copy(q, h, right, block):
        at = pl.ds(q * PAIR * TILE, PAIR * TILE)
        src = a_ref.at[at] if h == 0 and q * PAIR < n_raw else G.at[block, at]
        send, recv = (zr_send, zr_recv) if right else (zl_send, zl_recv)
        return pltpu.make_async_remote_copy(
            src_ref=src,
            dst_ref=G.at[block, at],
            send_sem=send.at[q, h],
            recv_sem=recv.at[q, h],
            device_id={"col": c + 1 if right else c - 1},
            device_id_type=MESH,
        )

    def z_wait(q, h):
        @pl.when(c - 1 - h >= 0)
        def _():
            z_copy(q, h, True, c - 1 - h).wait_recv()

        @pl.when(c + 1 + h < n_col)
        def _():
            z_copy(q, h, False, c + 1 + h).wait_recv()

    def z_edges(q, h, act):
        @pl.when((c - h >= 0) & (c < n_col - 1))
        def _():
            act(z_copy(q, h, True, c - h))

        @pl.when((c + h < n_col) & (c > 0))
        def _():
            act(z_copy(q, h, False, c + h))

    def z_hop(q, h):
        if h > 0:
            z_wait(q, h - 1)
        z_edges(q, h, lambda copy: copy.start())

    def order(s):
        far = list(range(1, bits))
        turn = s % len(far)
        return far[turn:] + far[:turn] + [0]

    def flip(s, b):
        return (own_ref[s] // 2**b) % 2 == 1

    def p_copy(s, i):
        b = order(s)[i]
        src = a_ref.at[rows(s)] if i == 0 else G.at[c, rows(s)]
        return pltpu.make_async_remote_copy(
            src_ref=src,
            dst_ref=X.at[i, rows(s - n_raw)],
            send_sem=p_send.at[s - n_raw, i],
            recv_sem=p_recv.at[s - n_raw, i],
            device_id={"row": partner(b)},
            device_id_type=MESH,
        )

    def p_stage(s, i):
        if i > 0:
            copy = p_copy(s, i - 1)
            copy.wait_recv()
            copy.wait_send()
            mine = a_ref[rows(s)] if i == 1 else G[c, rows(s)]
            G[c, rows(s)] = jnp.where(flip(s, order(s)[i - 1]), X[i - 1, rows(s - n_raw)], mine)
        if i < bits:
            p_copy(s, i).start()

    def r_copy(s, i):
        b = order(s)[i]
        src = G.at[:, rows(s)] if i == 0 else F.at[:, rows(s)]
        return pltpu.make_async_remote_copy(
            src_ref=src,
            dst_ref=RX.at[i, :, rows(s)],
            send_sem=r_send.at[s, i],
            recv_sem=r_recv.at[s, i],
            device_id={"row": partner(b)},
            device_id_type=MESH,
        )

    def r_stage(s, i):
        if i == 0:
            G[c, rows(s)] = a_ref[rows(s)]
        if i > 0:
            copy = r_copy(s, i - 1)
            copy.wait_recv()
            copy.wait_send()
            flipped = flip(s, order(s)[i - 1])
            for k in range(n_col):
                mine = G[k, rows(s)] if i == 1 else F[k, rows(s)]
                F[k, rows(s)] = jnp.where(flipped, RX[i - 1, k, rows(s)], mine)
        if i < bits:
            r_copy(s, i).start()

    def pack():
        count = jnp.int32(0)
        place = [jnp.int32(0)] * CAP
        for j in range(width_tiles):
            flag = scr_ref[0, j]
            for i in range(CAP):
                here = flag * (count == i).astype(jnp.int32)
                place[i] = place[i] + here * (j + 1)
            count = count + flag
        at = lax.broadcasted_iota(jnp.int32, (16, TILE), 0) + 1
        for i in range(CAP):
            total = jnp.zeros((TILE, TILE), jnp.float32)
            for j in range(width_tiles):
                block = amp_ref[:, j * TILE:(j + 1) * TILE].astype(jnp.float32)
                total = jnp.where(place[i] == j + 1, block, total)
            AG[p, i * TILE:(i + 1) * TILE] = total.astype(jnp.bfloat16)
            mark = jnp.where(at == place[i], 1.0, 0.0)
            AG[p, CAP * TILE + i * 16:CAP * TILE + (i + 1) * 16] = mark.astype(jnp.bfloat16)

    def a_copy(b):
        size = 2**b
        block = pl.ds((p // size) * size, size)
        return pltpu.make_async_remote_copy(
            src_ref=AG.at[block],
            dst_ref=AG.at[block],
            send_sem=a_send.at[b],
            recv_sem=a_recv.at[b],
            device_id={"row": partner(b)},
            device_id_type=MESH,
        )

    def a_wait(b):
        size = 2**b
        other = pl.ds((partner(b) // size) * size, size)
        pltpu.make_async_remote_copy(
            src_ref=AG.at[other],
            dst_ref=AG.at[other],
            send_sem=a_send.at[b],
            recv_sem=a_recv.at[b],
            device_id={"row": partner(b)},
            device_id_type=MESH,
        ).wait_recv()

    def expand():
        def step(k, carry):
            first = AG[k, 0:TILE].astype(jnp.float32)
            second = AG[k, TILE:2 * TILE].astype(jnp.float32)
            marks = AG[k, 2 * TILE:2 * TILE + 32].astype(jnp.float32)
            at = pl.ds(pl.multiple_of(k * TILE, TILE), TILE)
            for j in range(width_tiles):
                value = first * marks[j:j + 1] + second * marks[16 + j:17 + j]
                W[at, j * TILE:(j + 1) * TILE] = value.astype(jnp.bfloat16)
            return carry

        lax.fori_loop(0, n_row, step, 0)

    depth = a_ref.shape[1]

    wide = 2 * TILE
    kept = tiles // PAIR - 1

    def g_copy(k):
        at = pl.ds(kept * PAIR * TILE, PAIR * TILE)
        return pltpu.make_async_copy(G.at[k, at], g_out.at[:, pl.ds(k * depth, depth)], g_sem.at[k])

    def put(q):
        for k in range(n_col):
            g_copy(k).start()

    def o_copy(q):
        at = pl.ds(q * PAIR * TILE, PAIR * TILE)
        return pltpu.make_async_copy(O.at[at], part_out.at[at], o_sem.at[q])

    def compute(q):
        at = pl.ds(q * PAIR * TILE, PAIR * TILE)
        held = F if q * PAIR < n_raw else G

        def step(n, carry):
            cols = pl.ds(pl.multiple_of(n * wide, wide), wide)
            total = jnp.zeros((PAIR * TILE, wide), jnp.float32)
            for k in range(n_col):
                total += jnp.dot(
                    held[k, at], W[k * depth:(k + 1) * depth, cols], preferred_element_type=jnp.float32
                )
            O[at, cols] = total.astype(jnp.bfloat16)
            return carry

        lax.fori_loop(0, amp_ref.shape[1] // wide, step, 0)
        o_copy(q).start()

    w_copy = pltpu.make_async_copy(W, w_out, w_sem.at[0])

    last = n_col - 1
    pairs, raw_pairs = tiles // PAIR, n_raw // PAIR

    def pair(q):
        return range(q * PAIR, (q + 1) * PAIR)

    steps = []

    def at_place(place, step, *args):
        steps.append((place, len(steps), step, args))

    def a_stage(b):
        if b > 0:
            a_wait(b - 1)
        if b == 0:
            pack()
        if b < bits:
            a_copy(b).start()
        else:
            expand()
            w_copy.start()

    def own(q):
        if q >= raw_pairs:
            for s in pair(q):
                p_stage(s, bits)
        z_hop(q, 0)

    shift = 0.6 * (bits - 3)
    for q in range(pairs):
        j = q - raw_pairs
        if q < raw_pairs:
            at_place(0.0, own, q)
            at_place(2.6, z_wait, q, last - 1)
            at_place(6.9 + 1.7 * (bits - 3) + shift, compute, q)
        else:
            at_place((1.6 if j == 0 else 1.0 + 1.2 * j) + shift, own, q)
            at_place(4.4 + 1.5 * j + shift, z_wait, q, last - 1)
            if q == kept:
                at_place(4.4 + 1.5 * j + shift, put, q)
            else:
                at_place(5.35 + 1.6 * j + shift, compute, q)
        for h in range(1, last):
            if q < raw_pairs:
                at_place(0.75 + 0.95 * (h - 1), z_hop, q, h)
            else:
                at_place(2.7 + 1.3 * j + (0.9 + 0.2 * j) * (h - 1) + shift, z_hop, q, h)
        for s in pair(q):
            for i in range(bits + 1):
                if q < raw_pairs:
                    at_place(2.65 + 1.7 * i - (0.9 if i == bits else 0.0), r_stage, s, i)
                elif i < bits:
                    at_place(0.05 + 0.6 * i + 0.65 * j, p_stage, s, i)
    for b in range(bits + 1):
        at_place(0.1 if b == 0 else 1.75 + 0.9 * (b - 1), a_stage, b)
    for place, index, step, args in sorted(steps, key=lambda entry: entry[:2]):
        step(*args)

    for q in range(pairs):
        for h in range(last):
            z_edges(q, h, lambda copy: copy.wait_send())
    for b in range(bits):
        a_copy(b).wait_send()
    for k in range(n_col):
        g_copy(k).wait()
    for q in range(kept):
        o_copy(q).wait()
    w_copy.wait()


def finish(left_ref, right_ref, part_ref, out_ref):
    kept = part_ref.shape[0]
    out_ref[:kept] = part_ref[...]
    total = jnp.dot(left_ref[...], right_ref[...], preferred_element_type=jnp.float32)
    out_ref[kept:] = total.astype(out_ref.dtype)


def body(integrals, amplitudes, screen, next_owner):
    n_row, n_col = lax.axis_size("row"), lax.axis_size("col")
    bits = n_row.bit_length() - 1
    row_count, depth = integrals.shape
    width = amplitudes.shape[1]
    tiles = row_count // TILE
    n_raw = PAIR
    late = row_count - n_raw * TILE
    kept = row_count - PAIR * TILE
    last = n_col - 1
    dma = pltpu.SemaphoreType.DMA
    vmem = pl.BlockSpec(memory_space=pltpu.VMEM)
    smem = pl.BlockSpec(memory_space=pltpu.SMEM)
    bf16 = jnp.bfloat16
    gathered, screened, part = pl.pallas_call(
        functools.partial(kernel, n_row, n_col, n_raw),
        out_shape=[
            jax.ShapeDtypeStruct((PAIR * TILE, n_col * depth), bf16),
            jax.ShapeDtypeStruct((n_row * TILE, width), bf16),
            jax.ShapeDtypeStruct((kept, width), bf16),
        ],
        in_specs=[vmem, vmem, smem, smem],
        out_specs=[pl.BlockSpec(memory_space=pl.ANY)] * 3,
        scratch_shapes=[
            pltpu.VMEM((n_col, row_count, depth), bf16),
            pltpu.VMEM((bits, late, depth), bf16),
            pltpu.VMEM((n_col, n_raw * TILE, depth), bf16),
            pltpu.VMEM((bits, n_col, n_raw * TILE, depth), bf16),
            pltpu.VMEM((n_row, CAP * TILE + 32, TILE), bf16),
            pltpu.VMEM((n_row * TILE, width), bf16),
            pltpu.VMEM((kept, width), bf16),
            dma((tiles // PAIR, last)),
            dma((tiles // PAIR, last)),
            dma((tiles // PAIR, last)),
            dma((tiles // PAIR, last)),
            dma((tiles - n_raw, bits)),
            dma((tiles - n_raw, bits)),
            dma((n_raw, bits)),
            dma((n_raw, bits)),
            dma((bits,)),
            dma((bits,)),
            dma((n_col,)),
            dma((1,)),
            dma((tiles // PAIR - 1,)),
        ],
        compiler_params=pltpu.CompilerParams(
            collective_id=0, has_side_effects=True, vmem_limit_bytes=56 * 1024 * 1024
        ),
    )(integrals, amplitudes, screen, next_owner)
    wide = 2 * TILE
    return pl.pallas_call(
        finish,
        out_shape=jax.ShapeDtypeStruct((row_count, width), bf16),
        grid=(width // wide,),
        in_specs=[
            pl.BlockSpec(gathered.shape, lambda n: (0, 0)),
            pl.BlockSpec((screened.shape[0], wide), lambda n: (0, n)),
            pl.BlockSpec((kept, wide), lambda n: (0, n)),
        ],
        out_specs=pl.BlockSpec((row_count, wide), lambda n: (0, n)),
    )(gathered, screened, part)


def solution(mesh):
    placed = (P("row", "col"), P("row", "col"), P("row", "col"), P())
    return jax.shard_map(
        body, mesh=mesh, in_specs=placed, out_specs=P("row", "col"), check_vma=False
    )
```

```python
import functools

import jax
import jax.numpy as jnp
from jax import lax
from jax.experimental import pallas as pl
from jax.experimental.pallas import tpu as pltpu
from jax.sharding import PartitionSpec as P

TILE = 128
CAP = 2
PAIR = 2
MESH = pl.DeviceIdType.MESH


def kernel(
    n_row, n_col, n_raw,
    a_ref, amp_ref, scr_ref, own_ref, g_out, W, O,
    G, X, F, RX, AG,
    zr_send, zr_recv, zl_send, zl_recv, p_send, p_recv, r_send, r_recv, a_send, a_recv,
):
    p = lax.axis_index("row")
    c = lax.axis_index("col")
    bits = n_row.bit_length() - 1
    tiles = a_ref.shape[0] // TILE
    width_tiles = amp_ref.shape[1] // TILE

    def partner(b):
        mask = 2**b
        return p + mask - 2 * mask * ((p // mask) % 2)

    barrier = pltpu.get_barrier_semaphore()
    for b in range(bits):
        pl.semaphore_signal(barrier, inc=1, device_id={"row": partner(b)}, device_id_type=MESH)

    @pl.when(c > 0)
    def _():
        pl.semaphore_signal(barrier, inc=1, device_id={"col": c - 1}, device_id_type=MESH)

    @pl.when(c < n_col - 1)
    def _():
        pl.semaphore_signal(barrier, inc=1, device_id={"col": c + 1}, device_id_type=MESH)

    near = (c > 0).astype(jnp.int32) + (c < n_col - 1).astype(jnp.int32)
    pl.semaphore_wait(barrier, bits + near)

    def rows(s):
        return pl.ds(s * TILE, TILE)

    def z_copy(q, h, right, block):
        at = pl.ds(q * PAIR * TILE, PAIR * TILE)
        src = a_ref.at[at] if h == 0 and q * PAIR < n_raw else G.at[block, at]
        send, recv = (zr_send, zr_recv) if right else (zl_send, zl_recv)
        return pltpu.make_async_remote_copy(
            src_ref=src,
            dst_ref=G.at[block, at],
            send_sem=send.at[q, h],
            recv_sem=recv.at[q, h],
            device_id={"col": c + 1 if right else c - 1},
            device_id_type=MESH,
        )

    def z_wait(q, h):
        @pl.when(c - 1 - h >= 0)
        def _():
            z_copy(q, h, True, c - 1 - h).wait_recv()

        @pl.when(c + 1 + h < n_col)
        def _():
            z_copy(q, h, False, c + 1 + h).wait_recv()

    def z_edges(q, h, act):
        @pl.when((c - h >= 0) & (c < n_col - 1))
        def _():
            act(z_copy(q, h, True, c - h))

        @pl.when((c + h < n_col) & (c > 0))
        def _():
            act(z_copy(q, h, False, c + h))

    def z_hop(q, h):
        if h > 0:
            z_wait(q, h - 1)
        z_edges(q, h, lambda copy: copy.start())

    def order(s):
        far = list(range(1, bits))
        turn = s % len(far)
        return far[turn:] + far[:turn] + [0]

    def flip(s, b):
        return (own_ref[s] // 2**b) % 2 == 1

    def p_copy(s, i):
        b = order(s)[i]
        src = a_ref.at[rows(s)] if i == 0 else G.at[c, rows(s)]
        return pltpu.make_async_remote_copy(
            src_ref=src,
            dst_ref=X.at[i, rows(s - n_raw)],
            send_sem=p_send.at[s - n_raw, i],
            recv_sem=p_recv.at[s - n_raw, i],
            device_id={"row": partner(b)},
            device_id_type=MESH,
        )

    def p_stage(s, i):
        if i > 0:
            copy = p_copy(s, i - 1)
            copy.wait_recv()
            copy.wait_send()
            mine = a_ref[rows(s)] if i == 1 else G[c, rows(s)]
            G[c, rows(s)] = jnp.where(flip(s, order(s)[i - 1]), X[i - 1, rows(s - n_raw)], mine)
        if i < bits:
            p_copy(s, i).start()

    def r_copy(s, i):
        b = order(s)[i]
        src = G.at[:, rows(s)] if i == 0 else F.at[:, rows(s)]
        return pltpu.make_async_remote_copy(
            src_ref=src,
            dst_ref=RX.at[i, :, rows(s)],
            send_sem=r_send.at[s, i],
            recv_sem=r_recv.at[s, i],
            device_id={"row": partner(b)},
            device_id_type=MESH,
        )

    def r_stage(s, i):
        if i == 0:
            G[c, rows(s)] = a_ref[rows(s)]
        if i > 0:
            copy = r_copy(s, i - 1)
            copy.wait_recv()
            copy.wait_send()
            flipped = flip(s, order(s)[i - 1])
            for k in range(n_col):
                mine = G[k, rows(s)] if i == 1 else F[k, rows(s)]
                F[k, rows(s)] = jnp.where(flipped, RX[i - 1, k, rows(s)], mine)
        if i < bits:
            r_copy(s, i).start()

    def pack():
        count = jnp.int32(0)
        place = [jnp.int32(0)] * CAP
        for j in range(width_tiles):
            flag = scr_ref[0, j]
            for i in range(CAP):
                here = flag * (count == i).astype(jnp.int32)
                place[i] = place[i] + here * (j + 1)
            count = count + flag
        at = lax.broadcasted_iota(jnp.int32, (16, TILE), 0) + 1
        for i in range(CAP):
            total = jnp.zeros((TILE, TILE), jnp.float32)
            for j in range(width_tiles):
                block = amp_ref[:, j * TILE:(j + 1) * TILE].astype(jnp.float32)
                total = jnp.where(place[i] == j + 1, block, total)
            AG[p, i * TILE:(i + 1) * TILE] = total.astype(jnp.bfloat16)
            mark = jnp.where(at == place[i], 1.0, 0.0)
            AG[p, CAP * TILE + i * 16:CAP * TILE + (i + 1) * 16] = mark.astype(jnp.bfloat16)

    def a_copy(b):
        size = 2**b
        block = pl.ds((p // size) * size, size)
        return pltpu.make_async_remote_copy(
            src_ref=AG.at[block],
            dst_ref=AG.at[block],
            send_sem=a_send.at[b],
            recv_sem=a_recv.at[b],
            device_id={"row": partner(b)},
            device_id_type=MESH,
        )

    def a_wait(b):
        size = 2**b
        other = pl.ds((partner(b) // size) * size, size)
        pltpu.make_async_remote_copy(
            src_ref=AG.at[other],
            dst_ref=AG.at[other],
            send_sem=a_send.at[b],
            recv_sem=a_recv.at[b],
            device_id={"row": partner(b)},
            device_id_type=MESH,
        ).wait_recv()

    def expand():
        def step(k, carry):
            first = AG[k, 0:TILE].astype(jnp.float32)
            second = AG[k, TILE:2 * TILE].astype(jnp.float32)
            marks = AG[k, 2 * TILE:2 * TILE + 32].astype(jnp.float32)
            at = pl.ds(pl.multiple_of(k * TILE, TILE), TILE)
            for j in range(width_tiles):
                value = first * marks[j:j + 1] + second * marks[16 + j:17 + j]
                W[at, j * TILE:(j + 1) * TILE] = value.astype(jnp.bfloat16)
            return carry

        lax.fori_loop(0, n_row, step, 0)

    depth = a_ref.shape[1]

    wide = 2 * TILE
    kept = tiles // PAIR - 1

    def put(q):
        at = pl.ds(q * PAIR * TILE, PAIR * TILE)
        for k in range(n_col):
            g_out[:, k * depth:(k + 1) * depth] = G[k, at]

    def compute(q):
        at = pl.ds(q * PAIR * TILE, PAIR * TILE)
        held = F if q * PAIR < n_raw else G

        def step(n, carry):
            cols = pl.ds(pl.multiple_of(n * wide, wide), wide)
            total = jnp.zeros((PAIR * TILE, wide), jnp.float32)
            for k in range(n_col):
                total += jnp.dot(
                    held[k, at], W[k * depth:(k + 1) * depth, cols], preferred_element_type=jnp.float32
                )
            O[at, cols] = total.astype(jnp.bfloat16)
            return carry

        lax.fori_loop(0, amp_ref.shape[1] // wide, step, 0)

    last = n_col - 1
    pairs, raw_pairs = tiles // PAIR, n_raw // PAIR

    def pair(q):
        return range(q * PAIR, (q + 1) * PAIR)

    steps = []

    def at_place(place, step, *args):
        steps.append((place, len(steps), step, args))

    def a_stage(b):
        if b > 0:
            a_wait(b - 1)
        if b == 0:
            pack()
        if b < bits:
            a_copy(b).start()
        else:
            expand()

    def own(q):
        if q >= raw_pairs:
            for s in pair(q):
                p_stage(s, bits)
        z_hop(q, 0)

    shift = 0.6 * (bits - 3)
    for q in range(pairs):
        j = q - raw_pairs
        if q < raw_pairs:
            at_place(0.0, own, q)
            at_place(2.6, z_wait, q, last - 1)
            at_place(6.9 + 1.7 * (bits - 3) + shift, compute, q)
        else:
            at_place((1.6 if j == 0 else 1.0 + 1.2 * j) + shift, own, q)
            at_place(4.4 + 1.5 * j + shift, z_wait, q, last - 1)
            if q == kept:
                at_place(4.4 + 1.5 * j + shift, put, q)
            else:
                at_place(6.95 + 1.5 * (kept - raw_pairs - 2) + 0.01 * j + shift, compute, q)
        for h in range(1, last):
            if q < raw_pairs:
                at_place(0.75 + 0.95 * (h - 1), z_hop, q, h)
            else:
                at_place(2.7 + 1.3 * j + (0.9 + 0.2 * j) * (h - 1) + shift, z_hop, q, h)
        for s in pair(q):
            for i in range(bits + 1):
                if q < raw_pairs:
                    at_place(2.65 + 1.7 * i - (0.9 if i == bits else 0.0), r_stage, s, i)
                elif i < bits:
                    at_place(0.05 + 0.6 * i + 0.65 * j, p_stage, s, i)
    for b in range(bits + 1):
        at_place(0.1 if b == 0 else 1.75 + 0.9 * (b - 1), a_stage, b)
    for place, index, step, args in sorted(steps, key=lambda entry: entry[:2]):
        step(*args)

    for q in range(pairs):
        for h in range(last):
            z_edges(q, h, lambda copy: copy.wait_send())
    for b in range(bits):
        a_copy(b).wait_send()

def finish(left_ref, right_ref, part_ref, out_ref, held, sem):
    kept, width = part_ref.shape
    wide = 2 * TILE
    carry = pltpu.make_async_copy(part_ref, out_ref.at[pl.ds(0, kept)], sem.at[0])
    carry.start()

    def step(n, carried):
        cols = pl.ds(pl.multiple_of(n * wide, wide), wide)
        total = jnp.dot(left_ref[...], right_ref[:, cols], preferred_element_type=jnp.float32)
        held[:, cols] = total.astype(held.dtype)
        return carried

    lax.fori_loop(0, width // wide, step, 0)
    rest = pltpu.make_async_copy(held, out_ref.at[pl.ds(kept, held.shape[0])], sem.at[1])
    rest.start()
    carry.wait()
    rest.wait()


def body(integrals, amplitudes, screen, next_owner):
    n_row, n_col = lax.axis_size("row"), lax.axis_size("col")
    bits = n_row.bit_length() - 1
    row_count, depth = integrals.shape
    width = amplitudes.shape[1]
    tiles = row_count // TILE
    n_raw = PAIR
    late = row_count - n_raw * TILE
    kept = row_count - PAIR * TILE
    last = n_col - 1
    held = 2 * (PAIR * TILE * n_col * depth + n_row * TILE * width + kept * width)
    room = 63 * 1024 * 1024 + 512 * 1024 - held
    dma = pltpu.SemaphoreType.DMA
    vmem = pl.BlockSpec(memory_space=pltpu.VMEM)
    smem = pl.BlockSpec(memory_space=pltpu.SMEM)
    bf16 = jnp.bfloat16
    gathered, screened, part = pl.pallas_call(
        functools.partial(kernel, n_row, n_col, n_raw),
        out_shape=[
            pltpu.VMEM((PAIR * TILE, n_col * depth), bf16),
            pltpu.VMEM((n_row * TILE, width), bf16),
            pltpu.VMEM((kept, width), bf16),
        ],
        in_specs=[vmem, vmem, smem, smem],
        out_specs=[vmem] * 3,
        scratch_shapes=[
            pltpu.VMEM((n_col, row_count, depth), bf16),
            pltpu.VMEM((bits, late, depth), bf16),
            pltpu.VMEM((n_col, n_raw * TILE, depth), bf16),
            pltpu.VMEM((bits, n_col, n_raw * TILE, depth), bf16),
            pltpu.VMEM((n_row, CAP * TILE + 32, TILE), bf16),
            dma((tiles // PAIR, last)),
            dma((tiles // PAIR, last)),
            dma((tiles // PAIR, last)),
            dma((tiles // PAIR, last)),
            dma((tiles - n_raw, bits)),
            dma((tiles - n_raw, bits)),
            dma((n_raw, bits)),
            dma((n_raw, bits)),
            dma((bits,)),
            dma((bits,)),
        ],
        compiler_params=pltpu.CompilerParams(
            collective_id=0, has_side_effects=True, vmem_limit_bytes=room
        ),
    )(integrals, amplitudes, screen, next_owner)
    return pl.pallas_call(
        finish,
        out_shape=jax.ShapeDtypeStruct((row_count, width), bf16),
        in_specs=[vmem] * 3,
        out_specs=pl.BlockSpec(memory_space=pl.ANY),
        scratch_shapes=[pltpu.VMEM((row_count - kept, width), bf16), dma((2,))],
        compiler_params=pltpu.CompilerParams(vmem_limit_bytes=24 * 1024 * 1024),
    )(gathered, screened, part)


def solution(mesh):
    placed = (P("row", "col"), P("row", "col"), P("row", "col"), P())
    return jax.shard_map(
        body, mesh=mesh, in_specs=placed, out_specs=P("row", "col"), check_vma=False
    )
```

```python
import functools

import jax
import jax.numpy as jnp
from jax import lax
from jax.experimental import pallas as pl
from jax.experimental.pallas import tpu as pltpu
from jax.sharding import PartitionSpec as P

TILE = 128
CAP = 2
PAIR = 2
LEFT = 2
MESH = pl.DeviceIdType.MESH


def kernel(
    n_row, n_col, n_raw,
    a_ref, amp_ref, scr_ref, own_ref, g_out, W, O,
    G, X, F, RX, AG,
    zr_send, zr_recv, zl_send, zl_recv, p_send, p_recv, r_send, r_recv, a_send, a_recv,
):
    p = lax.axis_index("row")
    c = lax.axis_index("col")
    bits = n_row.bit_length() - 1
    tiles = a_ref.shape[0] // TILE
    width_tiles = amp_ref.shape[1] // TILE

    def partner(b):
        mask = 2**b
        return p + mask - 2 * mask * ((p // mask) % 2)

    barrier = pltpu.get_barrier_semaphore()
    for b in range(bits):
        pl.semaphore_signal(barrier, inc=1, device_id={"row": partner(b)}, device_id_type=MESH)

    @pl.when(c > 0)
    def _():
        pl.semaphore_signal(barrier, inc=1, device_id={"col": c - 1}, device_id_type=MESH)

    @pl.when(c < n_col - 1)
    def _():
        pl.semaphore_signal(barrier, inc=1, device_id={"col": c + 1}, device_id_type=MESH)

    near = (c > 0).astype(jnp.int32) + (c < n_col - 1).astype(jnp.int32)
    pl.semaphore_wait(barrier, bits + near)

    def rows(s):
        return pl.ds(s * TILE, TILE)

    def z_copy(q, h, right, block):
        at = pl.ds(q * PAIR * TILE, PAIR * TILE)
        src = a_ref.at[at] if h == 0 and q * PAIR < n_raw else G.at[block, at]
        send, recv = (zr_send, zr_recv) if right else (zl_send, zl_recv)
        return pltpu.make_async_remote_copy(
            src_ref=src,
            dst_ref=G.at[block, at],
            send_sem=send.at[q, h],
            recv_sem=recv.at[q, h],
            device_id={"col": c + 1 if right else c - 1},
            device_id_type=MESH,
        )

    def z_wait(q, h):
        @pl.when(c - 1 - h >= 0)
        def _():
            z_copy(q, h, True, c - 1 - h).wait_recv()

        @pl.when(c + 1 + h < n_col)
        def _():
            z_copy(q, h, False, c + 1 + h).wait_recv()

    def z_edges(q, h, act):
        @pl.when((c - h >= 0) & (c < n_col - 1))
        def _():
            act(z_copy(q, h, True, c - h))

        @pl.when((c + h < n_col) & (c > 0))
        def _():
            act(z_copy(q, h, False, c + h))

    def z_hop(q, h):
        if h > 0:
            z_wait(q, h - 1)
        z_edges(q, h, lambda copy: copy.start())

    def order(s):
        far = list(range(1, bits))
        turn = s % len(far)
        return far[turn:] + far[:turn] + [0]

    def flip(s, b):
        return (own_ref[s] // 2**b) % 2 == 1

    def p_copy(s, i):
        b = order(s)[i]
        src = a_ref.at[rows(s)] if i == 0 else G.at[c, rows(s)]
        return pltpu.make_async_remote_copy(
            src_ref=src,
            dst_ref=X.at[i, rows(s - n_raw)],
            send_sem=p_send.at[s - n_raw, i],
            recv_sem=p_recv.at[s - n_raw, i],
            device_id={"row": partner(b)},
            device_id_type=MESH,
        )

    def p_stage(s, i):
        if i > 0:
            copy = p_copy(s, i - 1)
            copy.wait_recv()
            copy.wait_send()
            mine = a_ref[rows(s)] if i == 1 else G[c, rows(s)]
            G[c, rows(s)] = jnp.where(flip(s, order(s)[i - 1]), X[i - 1, rows(s - n_raw)], mine)
        if i < bits:
            p_copy(s, i).start()

    def r_copy(s, i):
        b = order(s)[i]
        src = G.at[:, rows(s)] if i == 0 else F.at[:, rows(s)]
        return pltpu.make_async_remote_copy(
            src_ref=src,
            dst_ref=RX.at[i, :, rows(s)],
            send_sem=r_send.at[s, i],
            recv_sem=r_recv.at[s, i],
            device_id={"row": partner(b)},
            device_id_type=MESH,
        )

    def r_stage(s, i):
        if i == 0:
            G[c, rows(s)] = a_ref[rows(s)]
        if i > 0:
            copy = r_copy(s, i - 1)
            copy.wait_recv()
            copy.wait_send()
            flipped = flip(s, order(s)[i - 1])
            for k in range(n_col):
                mine = G[k, rows(s)] if i == 1 else F[k, rows(s)]
                F[k, rows(s)] = jnp.where(flipped, RX[i - 1, k, rows(s)], mine)
        if i < bits:
            r_copy(s, i).start()

    def pack():
        count = jnp.int32(0)
        place = [jnp.int32(0)] * CAP
        for j in range(width_tiles):
            flag = scr_ref[0, j]
            for i in range(CAP):
                here = flag * (count == i).astype(jnp.int32)
                place[i] = place[i] + here * (j + 1)
            count = count + flag
        at = lax.broadcasted_iota(jnp.int32, (16, TILE), 0) + 1
        for i in range(CAP):
            total = jnp.zeros((TILE, TILE), jnp.float32)
            for j in range(width_tiles):
                block = amp_ref[:, j * TILE:(j + 1) * TILE].astype(jnp.float32)
                total = jnp.where(place[i] == j + 1, block, total)
            AG[p, i * TILE:(i + 1) * TILE] = total.astype(jnp.bfloat16)
            mark = jnp.where(at == place[i], 1.0, 0.0)
            AG[p, CAP * TILE + i * 16:CAP * TILE + (i + 1) * 16] = mark.astype(jnp.bfloat16)

    def a_copy(b):
        size = 2**b
        block = pl.ds((p // size) * size, size)
        return pltpu.make_async_remote_copy(
            src_ref=AG.at[block],
            dst_ref=AG.at[block],
            send_sem=a_send.at[b],
            recv_sem=a_recv.at[b],
            device_id={"row": partner(b)},
            device_id_type=MESH,
        )

    def a_wait(b):
        size = 2**b
        other = pl.ds((partner(b) // size) * size, size)
        pltpu.make_async_remote_copy(
            src_ref=AG.at[other],
            dst_ref=AG.at[other],
            send_sem=a_send.at[b],
            recv_sem=a_recv.at[b],
            device_id={"row": partner(b)},
            device_id_type=MESH,
        ).wait_recv()

    def expand():
        def step(k, carry):
            first = AG[k, 0:TILE].astype(jnp.float32)
            second = AG[k, TILE:2 * TILE].astype(jnp.float32)
            marks = AG[k, 2 * TILE:2 * TILE + 32].astype(jnp.float32)
            at = pl.ds(pl.multiple_of(k * TILE, TILE), TILE)
            for j in range(width_tiles):
                value = first * marks[j:j + 1] + second * marks[16 + j:17 + j]
                W[at, j * TILE:(j + 1) * TILE] = value.astype(jnp.bfloat16)
            return carry

        lax.fori_loop(0, n_row, step, 0)

    depth = a_ref.shape[1]

    wide = 2 * TILE
    kept = tiles // PAIR - LEFT

    def put(q):
        at = pl.ds(q * PAIR * TILE, PAIR * TILE)
        to = pl.ds((q - kept) * PAIR * TILE, PAIR * TILE)
        for k in range(n_col):
            g_out[to, k * depth:(k + 1) * depth] = G[k, at]

    def compute(q):
        at = pl.ds(q * PAIR * TILE, PAIR * TILE)
        held = F if q * PAIR < n_raw else G

        def step(n, carry):
            cols = pl.ds(pl.multiple_of(n * wide, wide), wide)
            total = jnp.zeros((PAIR * TILE, wide), jnp.float32)
            for k in range(n_col):
                total += jnp.dot(
                    held[k, at], W[k * depth:(k + 1) * depth, cols], preferred_element_type=jnp.float32
                )
            O[at, cols] = total.astype(jnp.bfloat16)
            return carry

        lax.fori_loop(0, amp_ref.shape[1] // wide, step, 0)

    last = n_col - 1
    pairs, raw_pairs = tiles // PAIR, n_raw // PAIR

    def pair(q):
        return range(q * PAIR, (q + 1) * PAIR)

    steps = []

    def at_place(place, step, *args):
        steps.append((place, len(steps), step, args))

    def a_stage(b):
        if b > 0:
            a_wait(b - 1)
        if b == 0:
            pack()
        if b < bits:
            a_copy(b).start()
        else:
            expand()

    def own(q):
        if q >= raw_pairs:
            for s in pair(q):
                p_stage(s, bits)
        z_hop(q, 0)

    def compute_if(q, at_end):
        ends = (c == 0) | (c == n_col - 1)

        @pl.when(ends if at_end else jnp.logical_not(ends))
        def _():
            compute(q)

    shift = 0.6 * (bits - 3)
    for q in range(pairs):
        j = q - raw_pairs
        if q < raw_pairs:
            at_place(0.0, own, q)
            at_place(2.6, z_wait, q, last - 1)
            at_place(6.9 + 1.7 * (bits - 3) + shift, compute, q)
        else:
            at_place((1.6 if j == 0 else 1.0 + 1.2 * j) + shift, own, q)
            at_place(4.4 + 1.5 * j + shift, z_wait, q, last - 1)
            if q >= kept:
                at_place(4.4 + 1.5 * j + shift, put, q)
            else:
                at_place(4.45 + 1.5 * j + shift, compute_if, q, True)
                at_place(6.95 + 1.5 * (pairs - raw_pairs - 3) + 0.01 * j + shift, compute_if, q, False)
        for h in range(1, last):
            if q < raw_pairs:
                at_place(0.75 + 0.95 * (h - 1), z_hop, q, h)
            else:
                at_place(2.7 + 1.3 * j + (0.9 + 0.2 * j) * (h - 1) + shift, z_hop, q, h)
        for s in pair(q):
            for i in range(bits + 1):
                if q < raw_pairs:
                    at_place(2.65 + 1.7 * i - (0.9 if i == bits else 0.0), r_stage, s, i)
                elif i < bits:
                    at_place(0.05 + 0.6 * i + 0.65 * j, p_stage, s, i)
    for b in range(bits + 1):
        at_place(0.1 if b == 0 else 1.75 + 0.9 * (b - 1), a_stage, b)
    for place, index, step, args in sorted(steps, key=lambda entry: entry[:2]):
        step(*args)

    for q in range(pairs):
        for h in range(last):
            z_edges(q, h, lambda copy: copy.wait_send())
    for b in range(bits):
        a_copy(b).wait_send()

def finish(left_ref, right_ref, part_ref, out_ref, held, sem):
    kept, width = part_ref.shape
    wide = 2 * TILE
    carry = pltpu.make_async_copy(part_ref, out_ref.at[pl.ds(0, kept)], sem.at[0])
    carry.start()

    size = PAIR * TILE
    rests = []
    for q in range(LEFT):
        at = pl.ds(q * size, size)

        def step(n, carried):
            cols = pl.ds(pl.multiple_of(n * wide, wide), wide)
            total = jnp.dot(left_ref[at], right_ref[:, cols], preferred_element_type=jnp.float32)
            held[at, cols] = total.astype(held.dtype)
            return carried

        lax.fori_loop(0, width // wide, step, 0)
        rest = pltpu.make_async_copy(held.at[at], out_ref.at[pl.ds(kept + q * size, size)], sem.at[1 + q])
        rest.start()
        rests.append(rest)
    carry.wait()
    for rest in rests:
        rest.wait()


def body(integrals, amplitudes, screen, next_owner):
    n_row, n_col = lax.axis_size("row"), lax.axis_size("col")
    bits = n_row.bit_length() - 1
    row_count, depth = integrals.shape
    width = amplitudes.shape[1]
    tiles = row_count // TILE
    n_raw = PAIR
    late = row_count - n_raw * TILE
    kept = row_count - LEFT * PAIR * TILE
    last = n_col - 1
    held = 2 * (LEFT * PAIR * TILE * n_col * depth + n_row * TILE * width + kept * width)
    room = 63 * 1024 * 1024 + 512 * 1024 - held
    dma = pltpu.SemaphoreType.DMA
    vmem = pl.BlockSpec(memory_space=pltpu.VMEM)
    smem = pl.BlockSpec(memory_space=pltpu.SMEM)
    bf16 = jnp.bfloat16
    gathered, screened, part = pl.pallas_call(
        functools.partial(kernel, n_row, n_col, n_raw),
        out_shape=[
            pltpu.VMEM((LEFT * PAIR * TILE, n_col * depth), bf16),
            pltpu.VMEM((n_row * TILE, width), bf16),
            pltpu.VMEM((kept, width), bf16),
        ],
        in_specs=[vmem, vmem, smem, smem],
        out_specs=[vmem] * 3,
        scratch_shapes=[
            pltpu.VMEM((n_col, row_count, depth), bf16),
            pltpu.VMEM((bits, late, depth), bf16),
            pltpu.VMEM((n_col, n_raw * TILE, depth), bf16),
            pltpu.VMEM((bits, n_col, n_raw * TILE, depth), bf16),
            pltpu.VMEM((n_row, CAP * TILE + 32, TILE), bf16),
            dma((tiles // PAIR, last)),
            dma((tiles // PAIR, last)),
            dma((tiles // PAIR, last)),
            dma((tiles // PAIR, last)),
            dma((tiles - n_raw, bits)),
            dma((tiles - n_raw, bits)),
            dma((n_raw, bits)),
            dma((n_raw, bits)),
            dma((bits,)),
            dma((bits,)),
        ],
        compiler_params=pltpu.CompilerParams(
            collective_id=0, has_side_effects=True, vmem_limit_bytes=room
        ),
    )(integrals, amplitudes, screen, next_owner)
    return pl.pallas_call(
        finish,
        out_shape=jax.ShapeDtypeStruct((row_count, width), bf16),
        in_specs=[vmem] * 3,
        out_specs=pl.BlockSpec(memory_space=pl.ANY),
        scratch_shapes=[pltpu.VMEM((row_count - kept, width), bf16), dma((1 + LEFT,))],
        compiler_params=pltpu.CompilerParams(vmem_limit_bytes=24 * 1024 * 1024),
    )(gathered, screened, part)


def solution(mesh):
    placed = (P("row", "col"), P("row", "col"), P("row", "col"), P())
    return jax.shard_map(
        body, mesh=mesh, in_specs=placed, out_specs=P("row", "col"), check_vma=False
    )
```

```python
import functools

import jax
import jax.numpy as jnp
from jax import lax
from jax.experimental import pallas as pl
from jax.experimental.pallas import tpu as pltpu
from jax.sharding import PartitionSpec as P

TILE = 128
CAP = 2
PAIR = 2
LEFT = 1
MESH = pl.DeviceIdType.MESH


def kernel(
    n_row, n_col, n_raw,
    a_ref, amp_ref, scr_ref, own_ref, g_out, W, O,
    G, X, F, RX, AG,
    zr_send, zr_recv, zl_send, zl_recv, p_send, p_recv, r_send, r_recv, a_send, a_recv,
):
    p = lax.axis_index("row")
    c = lax.axis_index("col")
    bits = n_row.bit_length() - 1
    tiles = a_ref.shape[0] // TILE
    width_tiles = amp_ref.shape[1] // TILE

    def partner(b):
        mask = 2**b
        return p + mask - 2 * mask * ((p // mask) % 2)

    barrier = pltpu.get_barrier_semaphore()
    for b in range(bits):
        pl.semaphore_signal(barrier, inc=1, device_id={"row": partner(b)}, device_id_type=MESH)

    @pl.when(c > 0)
    def _():
        pl.semaphore_signal(barrier, inc=1, device_id={"col": c - 1}, device_id_type=MESH)

    @pl.when(c < n_col - 1)
    def _():
        pl.semaphore_signal(barrier, inc=1, device_id={"col": c + 1}, device_id_type=MESH)

    near = (c > 0).astype(jnp.int32) + (c < n_col - 1).astype(jnp.int32)
    pl.semaphore_wait(barrier, bits + near)

    def rows(s):
        return pl.ds(s * TILE, TILE)

    def z_copy(q, h, right, block):
        at = pl.ds(q * PAIR * TILE, PAIR * TILE)
        src = a_ref.at[at] if h == 0 and q * PAIR < n_raw else G.at[block, at]
        send, recv = (zr_send, zr_recv) if right else (zl_send, zl_recv)
        return pltpu.make_async_remote_copy(
            src_ref=src,
            dst_ref=G.at[block, at],
            send_sem=send.at[q, h],
            recv_sem=recv.at[q, h],
            device_id={"col": c + 1 if right else c - 1},
            device_id_type=MESH,
        )

    def z_wait(q, h):
        @pl.when(c - 1 - h >= 0)
        def _():
            z_copy(q, h, True, c - 1 - h).wait_recv()

        @pl.when(c + 1 + h < n_col)
        def _():
            z_copy(q, h, False, c + 1 + h).wait_recv()

    def z_edges(q, h, act):
        @pl.when((c - h >= 0) & (c < n_col - 1))
        def _():
            act(z_copy(q, h, True, c - h))

        @pl.when((c + h < n_col) & (c > 0))
        def _():
            act(z_copy(q, h, False, c + h))

    def z_hop(q, h):
        if h > 0:
            z_wait(q, h - 1)
        z_edges(q, h, lambda copy: copy.start())

    def order(s):
        far = list(range(1, bits))
        turn = s % len(far)
        return far[turn:] + far[:turn] + [0]

    def flip(s, b):
        return (own_ref[s] // 2**b) % 2 == 1

    def p_copy(s, i):
        b = order(s)[i]
        src = a_ref.at[rows(s)] if i == 0 else G.at[c, rows(s)]
        return pltpu.make_async_remote_copy(
            src_ref=src,
            dst_ref=X.at[i, rows(s - n_raw)],
            send_sem=p_send.at[s - n_raw, i],
            recv_sem=p_recv.at[s - n_raw, i],
            device_id={"row": partner(b)},
            device_id_type=MESH,
        )

    def p_stage(s, i):
        if i > 0:
            copy = p_copy(s, i - 1)
            copy.wait_recv()
            copy.wait_send()
            mine = a_ref[rows(s)] if i == 1 else G[c, rows(s)]
            G[c, rows(s)] = jnp.where(flip(s, order(s)[i - 1]), X[i - 1, rows(s - n_raw)], mine)
        if i < bits:
            p_copy(s, i).start()

    def r_copy(s, i):
        b = order(s)[i]
        src = G.at[:, rows(s)] if i == 0 else F.at[:, rows(s)]
        return pltpu.make_async_remote_copy(
            src_ref=src,
            dst_ref=RX.at[i, :, rows(s)],
            send_sem=r_send.at[s, i],
            recv_sem=r_recv.at[s, i],
            device_id={"row": partner(b)},
            device_id_type=MESH,
        )

    def r_stage(s, i):
        if i == 0:
            G[c, rows(s)] = a_ref[rows(s)]
        if i > 0:
            copy = r_copy(s, i - 1)
            copy.wait_recv()
            copy.wait_send()
            flipped = flip(s, order(s)[i - 1])
            for k in range(n_col):
                mine = G[k, rows(s)] if i == 1 else F[k, rows(s)]
                F[k, rows(s)] = jnp.where(flipped, RX[i - 1, k, rows(s)], mine)
        if i < bits:
            r_copy(s, i).start()

    def pack():
        count = jnp.int32(0)
        place = [jnp.int32(0)] * CAP
        for j in range(width_tiles):
            flag = scr_ref[0, j]
            for i in range(CAP):
                here = flag * (count == i).astype(jnp.int32)
                place[i] = place[i] + here * (j + 1)
            count = count + flag
        at = lax.broadcasted_iota(jnp.int32, (16, TILE), 0) + 1
        for i in range(CAP):
            total = jnp.zeros((TILE, TILE), jnp.float32)
            for j in range(width_tiles):
                block = amp_ref[:, j * TILE:(j + 1) * TILE].astype(jnp.float32)
                total = jnp.where(place[i] == j + 1, block, total)
            AG[p, i * TILE:(i + 1) * TILE] = total.astype(jnp.bfloat16)
            mark = jnp.where(at == place[i], 1.0, 0.0)
            AG[p, CAP * TILE + i * 16:CAP * TILE + (i + 1) * 16] = mark.astype(jnp.bfloat16)

    def a_copy(b):
        size = 2**b
        block = pl.ds((p // size) * size, size)
        return pltpu.make_async_remote_copy(
            src_ref=AG.at[block],
            dst_ref=AG.at[block],
            send_sem=a_send.at[b],
            recv_sem=a_recv.at[b],
            device_id={"row": partner(b)},
            device_id_type=MESH,
        )

    def a_wait(b):
        size = 2**b
        other = pl.ds((partner(b) // size) * size, size)
        pltpu.make_async_remote_copy(
            src_ref=AG.at[other],
            dst_ref=AG.at[other],
            send_sem=a_send.at[b],
            recv_sem=a_recv.at[b],
            device_id={"row": partner(b)},
            device_id_type=MESH,
        ).wait_recv()

    def expand():
        def step(k, carry):
            first = AG[k, 0:TILE].astype(jnp.float32)
            second = AG[k, TILE:2 * TILE].astype(jnp.float32)
            marks = AG[k, 2 * TILE:2 * TILE + 32].astype(jnp.float32)
            at = pl.ds(pl.multiple_of(k * TILE, TILE), TILE)
            for j in range(width_tiles):
                value = first * marks[j:j + 1] + second * marks[16 + j:17 + j]
                W[at, j * TILE:(j + 1) * TILE] = value.astype(jnp.bfloat16)
            return carry

        lax.fori_loop(0, n_row, step, 0)

    depth = a_ref.shape[1]

    wide = 2 * TILE
    kept = tiles // PAIR - LEFT

    def put(q):
        at = pl.ds(q * PAIR * TILE, PAIR * TILE)
        to = pl.ds((q - kept) * PAIR * TILE, PAIR * TILE)
        for k in range(n_col):
            g_out[to, k * depth:(k + 1) * depth] = G[k, at]

    def compute(q):
        at = pl.ds(q * PAIR * TILE, PAIR * TILE)
        held = F if q * PAIR < n_raw else G

        def step(n, carry):
            cols = pl.ds(pl.multiple_of(n * wide, wide), wide)
            total = jnp.zeros((PAIR * TILE, wide), jnp.float32)
            for k in range(n_col):
                total += jnp.dot(
                    held[k, at], W[k * depth:(k + 1) * depth, cols], preferred_element_type=jnp.float32
                )
            O[at, cols] = total.astype(jnp.bfloat16)
            return carry

        lax.fori_loop(0, amp_ref.shape[1] // wide, step, 0)

    last = n_col - 1
    pairs, raw_pairs = tiles // PAIR, n_raw // PAIR

    def pair(q):
        return range(q * PAIR, (q + 1) * PAIR)

    steps = []

    def at_place(place, step, *args):
        steps.append((place, len(steps), step, args))

    def a_stage(b):
        if b > 0:
            a_wait(b - 1)
        if b == 0:
            pack()
        if b < bits:
            a_copy(b).start()
        else:
            expand()

    def own(q):
        if q >= raw_pairs:
            for s in pair(q):
                p_stage(s, bits)
        z_hop(q, 0)

    def compute_if(q, at_end):
        ends = (c == 0) | (c == n_col - 1)

        @pl.when(ends if at_end else jnp.logical_not(ends))
        def _():
            compute(q)

    shift = 0.6 * (bits - 3)
    for q in range(pairs):
        j = q - raw_pairs
        if q < raw_pairs:
            at_place(0.0, own, q)
            at_place(2.6, z_wait, q, last - 1)
            at_place(6.9 + 1.7 * (bits - 3) + shift, compute, q)
        else:
            at_place((1.6 if j == 0 else 1.0 + 1.2 * j) + shift, own, q)
            at_place(4.4 + 1.5 * j + shift, z_wait, q, last - 1)
            if q >= kept:
                at_place(4.4 + 1.5 * j + shift, put, q)
            else:
                at_place(4.45 + 1.5 * j + shift, compute_if, q, True)
                at_place(6.95 + 1.5 * (pairs - raw_pairs - 3) + 0.01 * j + shift, compute_if, q, False)
        for h in range(1, last):
            if q < raw_pairs:
                at_place(0.75 + 0.95 * (h - 1), z_hop, q, h)
            else:
                at_place(2.7 + 1.3 * j + (0.9 + 0.2 * j) * (h - 1) + shift, z_hop, q, h)
        for s in pair(q):
            for i in range(bits + 1):
                if q < raw_pairs:
                    at_place(2.65 + 1.7 * i - (0.9 if i == bits else 0.0), r_stage, s, i)
                elif i < bits:
                    at_place(0.05 + 0.6 * i + 0.65 * j, p_stage, s, i)
    for b in range(bits + 1):
        at_place(0.1 if b == 0 else 1.75 + 0.9 * (b - 1), a_stage, b)
    for place, index, step, args in sorted(steps, key=lambda entry: entry[:2]):
        step(*args)

    for q in range(pairs):
        for h in range(last):
            z_edges(q, h, lambda copy: copy.wait_send())
    for b in range(bits):
        a_copy(b).wait_send()

def finish(left_ref, right_ref, part_ref, out_ref, held, sem):
    kept, width = part_ref.shape
    wide = 2 * TILE
    carry = pltpu.make_async_copy(part_ref, out_ref.at[pl.ds(0, kept)], sem.at[0])
    carry.start()

    size = PAIR * TILE
    rests = []
    for q in range(LEFT):
        at = pl.ds(q * size, size)

        def step(n, carried):
            cols = pl.ds(pl.multiple_of(n * wide, wide), wide)
            total = jnp.dot(left_ref[at], right_ref[:, cols], preferred_element_type=jnp.float32)
            held[at, cols] = total.astype(held.dtype)
            return carried

        lax.fori_loop(0, width // wide, step, 0)
        rest = pltpu.make_async_copy(held.at[at], out_ref.at[pl.ds(kept + q * size, size)], sem.at[1 + q])
        rest.start()
        rests.append(rest)
    carry.wait()
    for rest in rests:
        rest.wait()


def body(integrals, amplitudes, screen, next_owner):
    n_row, n_col = lax.axis_size("row"), lax.axis_size("col")
    bits = n_row.bit_length() - 1
    row_count, depth = integrals.shape
    width = amplitudes.shape[1]
    tiles = row_count // TILE
    n_raw = PAIR
    late = row_count - n_raw * TILE
    kept = row_count - LEFT * PAIR * TILE
    last = n_col - 1
    held = 2 * (LEFT * PAIR * TILE * n_col * depth + n_row * TILE * width + kept * width)
    room = 63 * 1024 * 1024 + 512 * 1024 - held
    dma = pltpu.SemaphoreType.DMA
    vmem = pl.BlockSpec(memory_space=pltpu.VMEM)
    smem = pl.BlockSpec(memory_space=pltpu.SMEM)
    bf16 = jnp.bfloat16
    gathered, screened, part = pl.pallas_call(
        functools.partial(kernel, n_row, n_col, n_raw),
        out_shape=[
            pltpu.VMEM((LEFT * PAIR * TILE, n_col * depth), bf16),
            pltpu.VMEM((n_row * TILE, width), bf16),
            pltpu.VMEM((kept, width), bf16),
        ],
        in_specs=[vmem, vmem, smem, smem],
        out_specs=[vmem] * 3,
        scratch_shapes=[
            pltpu.VMEM((n_col, row_count, depth), bf16),
            pltpu.VMEM((bits, late, depth), bf16),
            pltpu.VMEM((n_col, n_raw * TILE, depth), bf16),
            pltpu.VMEM((bits, n_col, n_raw * TILE, depth), bf16),
            pltpu.VMEM((n_row, CAP * TILE + 32, TILE), bf16),
            dma((tiles // PAIR, last)),
            dma((tiles // PAIR, last)),
            dma((tiles // PAIR, last)),
            dma((tiles // PAIR, last)),
            dma((tiles - n_raw, bits)),
            dma((tiles - n_raw, bits)),
            dma((n_raw, bits)),
            dma((n_raw, bits)),
            dma((bits,)),
            dma((bits,)),
        ],
        compiler_params=pltpu.CompilerParams(
            collective_id=0, has_side_effects=True, vmem_limit_bytes=room
        ),
    )(integrals, amplitudes, screen, next_owner)
    return pl.pallas_call(
        finish,
        out_shape=jax.ShapeDtypeStruct((row_count, width), bf16),
        in_specs=[vmem] * 3,
        out_specs=pl.BlockSpec(memory_space=pl.ANY),
        scratch_shapes=[pltpu.VMEM((row_count - kept, width), bf16), dma((1 + LEFT,))],
        compiler_params=pltpu.CompilerParams(vmem_limit_bytes=24 * 1024 * 1024),
    )(gathered, screened, part)


def solution(mesh):
    placed = (P("row", "col"), P("row", "col"), P("row", "col"), P())
    return jax.shard_map(
        body, mesh=mesh, in_specs=placed, out_specs=P("row", "col"), check_vma=False
    )
```

```python
import functools

import jax
import jax.numpy as jnp
from jax import lax
from jax.experimental import pallas as pl
from jax.experimental.pallas import tpu as pltpu
from jax.sharding import PartitionSpec as P

TILE = 128
CAP = 2
PAIR = 2
LEFT = 1
MESH = pl.DeviceIdType.MESH


def kernel(
    n_row, n_col, n_raw,
    a_ref, amp_ref, scr_ref, own_ref, g_out, W, O,
    G, X, F, RX, AG,
    zr_send, zr_recv, zl_send, zl_recv, p_send, p_recv, r_send, r_recv, a_send, a_recv,
):
    p = lax.axis_index("row")
    c = lax.axis_index("col")
    bits = n_row.bit_length() - 1
    tiles = a_ref.shape[0] // TILE
    width_tiles = amp_ref.shape[1] // TILE

    def partner(b):
        mask = 2**b
        return p + mask - 2 * mask * ((p // mask) % 2)

    barrier = pltpu.get_barrier_semaphore()
    for b in range(bits):
        pl.semaphore_signal(barrier, inc=1, device_id={"row": partner(b)}, device_id_type=MESH)

    @pl.when(c > 0)
    def _():
        pl.semaphore_signal(barrier, inc=1, device_id={"col": c - 1}, device_id_type=MESH)

    @pl.when(c < n_col - 1)
    def _():
        pl.semaphore_signal(barrier, inc=1, device_id={"col": c + 1}, device_id_type=MESH)

    near = (c > 0).astype(jnp.int32) + (c < n_col - 1).astype(jnp.int32)
    pl.semaphore_wait(barrier, bits + near)

    def rows(s):
        return pl.ds(s * TILE, TILE)

    def z_copy(q, h, right, block):
        at = pl.ds(q * PAIR * TILE, PAIR * TILE)
        src = a_ref.at[at] if h == 0 and q * PAIR < n_raw else G.at[block, at]
        send, recv = (zr_send, zr_recv) if right else (zl_send, zl_recv)
        return pltpu.make_async_remote_copy(
            src_ref=src,
            dst_ref=G.at[block, at],
            send_sem=send.at[q, h],
            recv_sem=recv.at[q, h],
            device_id={"col": c + 1 if right else c - 1},
            device_id_type=MESH,
        )

    def z_wait(q, h):
        @pl.when(c - 1 - h >= 0)
        def _():
            z_copy(q, h, True, c - 1 - h).wait_recv()

        @pl.when(c + 1 + h < n_col)
        def _():
            z_copy(q, h, False, c + 1 + h).wait_recv()

    def z_edges(q, h, act):
        @pl.when((c - h >= 0) & (c < n_col - 1))
        def _():
            act(z_copy(q, h, True, c - h))

        @pl.when((c + h < n_col) & (c > 0))
        def _():
            act(z_copy(q, h, False, c + h))

    def z_hop(q, h):
        if h > 0:
            z_wait(q, h - 1)
        z_edges(q, h, lambda copy: copy.start())

    def order(s):
        far = list(range(1, bits))
        turn = s % len(far)
        return far[turn:] + far[:turn] + [0]

    def flip(s, b):
        return (own_ref[s] // 2**b) % 2 == 1

    def p_copy(s, i):
        b = order(s)[i]
        src = a_ref.at[rows(s)] if i == 0 else G.at[c, rows(s)]
        return pltpu.make_async_remote_copy(
            src_ref=src,
            dst_ref=X.at[i, rows(s - n_raw)],
            send_sem=p_send.at[s - n_raw, i],
            recv_sem=p_recv.at[s - n_raw, i],
            device_id={"row": partner(b)},
            device_id_type=MESH,
        )

    def p_stage(s, i):
        if i > 0:
            copy = p_copy(s, i - 1)
            copy.wait_recv()
            copy.wait_send()
            mine = a_ref[rows(s)] if i == 1 else G[c, rows(s)]
            G[c, rows(s)] = jnp.where(flip(s, order(s)[i - 1]), X[i - 1, rows(s - n_raw)], mine)
        if i < bits:
            p_copy(s, i).start()

    def r_copy(s, i):
        b = order(s)[i]
        src = G.at[:, rows(s)] if i == 0 else F.at[:, rows(s)]
        return pltpu.make_async_remote_copy(
            src_ref=src,
            dst_ref=RX.at[i, :, rows(s)],
            send_sem=r_send.at[s, i],
            recv_sem=r_recv.at[s, i],
            device_id={"row": partner(b)},
            device_id_type=MESH,
        )

    def r_stage(s, i):
        if i == 0:
            G[c, rows(s)] = a_ref[rows(s)]
        if i > 0:
            copy = r_copy(s, i - 1)
            copy.wait_recv()
            copy.wait_send()
            flipped = flip(s, order(s)[i - 1])
            for k in range(n_col):
                mine = G[k, rows(s)] if i == 1 else F[k, rows(s)]
                F[k, rows(s)] = jnp.where(flipped, RX[i - 1, k, rows(s)], mine)
        if i < bits:
            r_copy(s, i).start()

    def pack():
        count = jnp.int32(0)
        place = [jnp.int32(0)] * CAP
        for j in range(width_tiles):
            flag = scr_ref[0, j]
            for i in range(CAP):
                here = flag * (count == i).astype(jnp.int32)
                place[i] = place[i] + here * (j + 1)
            count = count + flag
        at = lax.broadcasted_iota(jnp.int32, (16, TILE), 0) + 1
        for i in range(CAP):
            total = jnp.zeros((TILE, TILE), jnp.float32)
            for j in range(width_tiles):
                block = amp_ref[:, j * TILE:(j + 1) * TILE].astype(jnp.float32)
                total = jnp.where(place[i] == j + 1, block, total)
            AG[p, i * TILE:(i + 1) * TILE] = total.astype(jnp.bfloat16)
            mark = jnp.where(at == place[i], 1.0, 0.0)
            AG[p, CAP * TILE + i * 16:CAP * TILE + (i + 1) * 16] = mark.astype(jnp.bfloat16)

    def a_copy(b):
        size = 2**b
        block = pl.ds((p // size) * size, size)
        return pltpu.make_async_remote_copy(
            src_ref=AG.at[block],
            dst_ref=AG.at[block],
            send_sem=a_send.at[b],
            recv_sem=a_recv.at[b],
            device_id={"row": partner(b)},
            device_id_type=MESH,
        )

    def a_wait(b):
        size = 2**b
        other = pl.ds((partner(b) // size) * size, size)
        pltpu.make_async_remote_copy(
            src_ref=AG.at[other],
            dst_ref=AG.at[other],
            send_sem=a_send.at[b],
            recv_sem=a_recv.at[b],
            device_id={"row": partner(b)},
            device_id_type=MESH,
        ).wait_recv()

    def expand():
        def step(k, carry):
            first = AG[k, 0:TILE].astype(jnp.float32)
            second = AG[k, TILE:2 * TILE].astype(jnp.float32)
            marks = AG[k, 2 * TILE:2 * TILE + 32].astype(jnp.float32)
            at = pl.ds(pl.multiple_of(k * TILE, TILE), TILE)
            for j in range(width_tiles):
                value = first * marks[j:j + 1] + second * marks[16 + j:17 + j]
                W[at, j * TILE:(j + 1) * TILE] = value.astype(jnp.bfloat16)
            return carry

        lax.fori_loop(0, n_row, step, 0)

    depth = a_ref.shape[1]

    wide = 2 * TILE
    kept = tiles // PAIR - LEFT

    def put(q):
        at = pl.ds(q * PAIR * TILE, PAIR * TILE)
        to = pl.ds((q - kept) * PAIR * TILE, PAIR * TILE)
        for k in range(n_col):
            g_out[to, k * depth:(k + 1) * depth] = G[k, at]

    def compute(q):
        at = pl.ds(q * PAIR * TILE, PAIR * TILE)
        held = F if q * PAIR < n_raw else G

        def step(n, carry):
            cols = pl.ds(pl.multiple_of(n * wide, wide), wide)
            total = jnp.zeros((PAIR * TILE, wide), jnp.float32)
            for k in range(n_col):
                total += jnp.dot(
                    held[k, at], W[k * depth:(k + 1) * depth, cols], preferred_element_type=jnp.float32
                )
            O[at, cols] = total.astype(jnp.bfloat16)
            return carry

        lax.fori_loop(0, amp_ref.shape[1] // wide, step, 0)

    last = n_col - 1
    pairs, raw_pairs = tiles // PAIR, n_raw // PAIR

    def pair(q):
        return range(q * PAIR, (q + 1) * PAIR)

    steps = []

    def at_place(place, step, *args):
        steps.append((place, len(steps), step, args))

    def a_stage(b):
        if b > 0:
            a_wait(b - 1)
        if b == 0:
            pack()
        if b < bits:
            a_copy(b).start()
        else:
            expand()

    def own(q):
        if q >= raw_pairs:
            for s in pair(q):
                p_stage(s, bits)
        z_hop(q, 0)

    def compute_if(q, at_end):
        ends = (c == 0) | (c == n_col - 1)

        @pl.when(ends if at_end else jnp.logical_not(ends))
        def _():
            compute(q)

    shift = 0.6 * (bits - 3)
    for q in range(pairs):
        j = q - raw_pairs
        if q < raw_pairs:
            at_place(0.0, own, q)
            at_place(2.6, z_wait, q, last - 1)
            at_place(2.65 + 1.37 * (bits - 1) + 0.42, compute_if, q, True)
            at_place(6.9 + 1.7 * (bits - 3) + shift, compute_if, q, False)
        else:
            at_place((1.6 if j == 0 else 1.0 + 1.2 * j) + shift, own, q)
            at_place(4.4 + 1.5 * j + shift, z_wait, q, last - 1)
            if q >= kept:
                at_place(4.4 + 1.5 * j + shift, put, q)
            else:
                at_place(4.45 + 1.5 * j + shift, compute_if, q, True)
                at_place(6.95 + 1.5 * (pairs - raw_pairs - 3) + 0.01 * j + shift, compute_if, q, False)
        for h in range(1, last):
            if q < raw_pairs:
                at_place(0.75 + 0.95 * (h - 1), z_hop, q, h)
            else:
                at_place(2.7 + 1.3 * j + (0.9 + 0.2 * j) * (h - 1) + shift, z_hop, q, h)
        for s in pair(q):
            for i in range(bits + 1):
                if q < raw_pairs:
                    at_place(2.65 + 1.37 * i - (0.97 if i == bits else 0.0), r_stage, s, i)
                elif i < bits:
                    at_place(0.05 + 0.6 * i + 0.65 * j, p_stage, s, i)
    for b in range(bits + 1):
        at_place(0.1 if b == 0 else 1.75 + 0.9 * (b - 1), a_stage, b)
    for place, index, step, args in sorted(steps, key=lambda entry: entry[:2]):
        step(*args)

    for q in range(pairs):
        for h in range(last):
            z_edges(q, h, lambda copy: copy.wait_send())
    for b in range(bits):
        a_copy(b).wait_send()

def finish(left_ref, right_ref, part_ref, out_ref, held, sem):
    kept, width = part_ref.shape
    wide = 2 * TILE
    carry = pltpu.make_async_copy(part_ref, out_ref.at[pl.ds(0, kept)], sem.at[0])
    carry.start()

    size = PAIR * TILE
    rests = []
    for q in range(LEFT):
        at = pl.ds(q * size, size)

        def step(n, carried):
            cols = pl.ds(pl.multiple_of(n * wide, wide), wide)
            total = jnp.dot(left_ref[at], right_ref[:, cols], preferred_element_type=jnp.float32)
            held[at, cols] = total.astype(held.dtype)
            return carried

        lax.fori_loop(0, width // wide, step, 0)
        rest = pltpu.make_async_copy(held.at[at], out_ref.at[pl.ds(kept + q * size, size)], sem.at[1 + q])
        rest.start()
        rests.append(rest)
    carry.wait()
    for rest in rests:
        rest.wait()


def body(integrals, amplitudes, screen, next_owner):
    n_row, n_col = lax.axis_size("row"), lax.axis_size("col")
    bits = n_row.bit_length() - 1
    row_count, depth = integrals.shape
    width = amplitudes.shape[1]
    tiles = row_count // TILE
    n_raw = PAIR
    late = row_count - n_raw * TILE
    kept = row_count - LEFT * PAIR * TILE
    last = n_col - 1
    held = 2 * (LEFT * PAIR * TILE * n_col * depth + n_row * TILE * width + kept * width)
    room = 63 * 1024 * 1024 + 512 * 1024 - held
    dma = pltpu.SemaphoreType.DMA
    vmem = pl.BlockSpec(memory_space=pltpu.VMEM)
    smem = pl.BlockSpec(memory_space=pltpu.SMEM)
    bf16 = jnp.bfloat16
    gathered, screened, part = pl.pallas_call(
        functools.partial(kernel, n_row, n_col, n_raw),
        out_shape=[
            pltpu.VMEM((LEFT * PAIR * TILE, n_col * depth), bf16),
            pltpu.VMEM((n_row * TILE, width), bf16),
            pltpu.VMEM((kept, width), bf16),
        ],
        in_specs=[vmem, vmem, smem, smem],
        out_specs=[vmem] * 3,
        scratch_shapes=[
            pltpu.VMEM((n_col, row_count, depth), bf16),
            pltpu.VMEM((bits, late, depth), bf16),
            pltpu.VMEM((n_col, n_raw * TILE, depth), bf16),
            pltpu.VMEM((bits, n_col, n_raw * TILE, depth), bf16),
            pltpu.VMEM((n_row, CAP * TILE + 32, TILE), bf16),
            dma((tiles // PAIR, last)),
            dma((tiles // PAIR, last)),
            dma((tiles // PAIR, last)),
            dma((tiles // PAIR, last)),
            dma((tiles - n_raw, bits)),
            dma((tiles - n_raw, bits)),
            dma((n_raw, bits)),
            dma((n_raw, bits)),
            dma((bits,)),
            dma((bits,)),
        ],
        compiler_params=pltpu.CompilerParams(
            collective_id=0, has_side_effects=True, vmem_limit_bytes=room
        ),
    )(integrals, amplitudes, screen, next_owner)
    return pl.pallas_call(
        finish,
        out_shape=jax.ShapeDtypeStruct((row_count, width), bf16),
        in_specs=[vmem] * 3,
        out_specs=pl.BlockSpec(memory_space=pl.ANY),
        scratch_shapes=[pltpu.VMEM((row_count - kept, width), bf16), dma((1 + LEFT,))],
        compiler_params=pltpu.CompilerParams(vmem_limit_bytes=24 * 1024 * 1024),
    )(gathered, screened, part)


def solution(mesh):
    placed = (P("row", "col"), P("row", "col"), P("row", "col"), P())
    return jax.shard_map(
        body, mesh=mesh, in_specs=placed, out_specs=P("row", "col"), check_vma=False
    )
```
